256 devices in a mesh: orb: 64 (over x, z, core), rep: 4 (over y).
Axes of the slice: x: 4, y: 4, z: 8, core: 2. Of those that a mesh axis runs over, the one named last changes fastest.
Arguments:
- ints_block: bfloat16 [512, 1536, 512], P('orb', 'rep'), may hold values from -6 to 6
- pair_vectors: bfloat16 [6144, 2, 40, 512], P('orb'), may hold values from -0.0390625 to 0.0390625
- pair_orbitals: int32 [6144, 2], P('orb'), may hold values from 0 to 511, as said below
- orbital_place: int32 [512], replicated, may hold values from 0 to 511, as said below
- amplitudes: bfloat16 [6144, 1600], P(('orb', 'rep')), may hold values from -3 to 3
- pno_energy: float32 [6144, 40], P(('orb', 'rep')), may hold values from 0.2 to 3
- occupied_fock_diagonal: float32 [512], replicated, may hold values from -2 to -0.3
Outputs:
- residual: float32 [6144, 1600], P(('orb', 'rep'))
The draws below stay inside these ranges and needn't reach their ends.
Inputs may be any that keep to these rules, and one draw needn't show every extreme that they name: `pair_orbitals`: within the 96 pairs of one index of orb, at most 4 of the 192 orbital entries have their block on one owner (owner = orbital_place // 8); some owner has exactly 4 entries from the pairs of every index of orb. `orbital_place`: A permutation of the orbitals.
All inputs are finite; a program needn't handle non-finite values.
Results may differ from the reference program's by a relative error of at most 0.0028.
Values may be sent and summed in bfloat16 or wider, within the bound.
No kernel may reach another device: no remote copies, remote signals or barrier semaphores. Data moves between devices by JAX's collectives and lax.ppermute only.
A program may use at most 128 MiB of HBM per device.

```python
import jax
import jax.numpy as jnp
from jax import lax

NPNO = 40
NAUX = 1536
NPAO = 512
ORB_DEV = 8
PAIR_DEV = 96
NORB = 512
PAIRS = 6144
CAP = 4
N_ORB = 64


def pair_lookup(key):
    place = jax.random.permutation(jax.random.fold_in(key, 11), NORB).astype(jnp.int32)
    inverse = jnp.argsort(place).astype(jnp.int32)
    busiest_holder = jax.random.randint(jax.random.fold_in(key, 12), (), 0, N_ORB)
    halves = 2 * PAIR_DEV

    def one_source(source):
        local_key = jax.random.fold_in(jax.random.fold_in(key, 13), source)
        spread = jax.random.permutation(jax.random.fold_in(local_key, 1), (N_ORB - 1) * CAP)[:halves - CAP]
        others = spread // CAP
        others = others + (others >= busiest_holder).astype(others.dtype)
        owners = jnp.concatenate([jnp.full((CAP,), busiest_holder, others.dtype), others])
        rows = jax.random.randint(jax.random.fold_in(local_key, 2), (halves,), 0, ORB_DEV)
        order = jax.random.permutation(jax.random.fold_in(local_key, 3), halves)
        return (owners * ORB_DEV + rows)[order].astype(jnp.int32)
    positions = jax.vmap(one_source)(jnp.arange(N_ORB))
    orbitals = inverse[positions].reshape(N_ORB * PAIR_DEV, 2).astype(jnp.int32)
    return (place, orbitals)


def draw_pair_orbitals(key, part):
    place, orbitals = pair_lookup(key)
    return orbitals


def draw_orbital_place(key, part):
    place, orbitals = pair_lookup(key)
    return place


def steps_of(rng, shape, pieces, smallest, high):
    factor_of, own = 1.0, jax.random.fold_in(rng, 6)
    for axis_at, shards_of in pieces:
        heights = jnp.exp(jax.random.uniform(jax.random.fold_in(own, axis_at), (shards_of,), jnp.float32, smallest / len(pieces), high / len(pieces)))
        factor_of = factor_of * jnp.repeat(heights, shape[axis_at] // shards_of).reshape([-1 if axis == axis_at else 1 for axis in range(len(shape))])
    return factor_of


def centred(key, dims, scale, most, cuts=(), held_as=jnp.bfloat16):
    values = jax.random.normal(key, dims, jnp.float32) * scale
    if len(cuts) > 0:
        values = steps_of(key, dims, cuts, -0.22, 0.18) * values
    return jnp.clip(values, min=-most, max=most).astype(held_as)


def setup_inputs(seed: int = 0) -> dict:
    key_list = jax.random.split(jax.random.key(seed), 8)
    return {
        "ints_block": centred(key_list[0], (NORB, NAUX, NPAO), 1.0, 6.0, ((0, 64), (1, 4))),
        "pair_vectors": centred(key_list[1], (PAIRS, 2, NPNO, NPAO), (NPAO * 39) ** -0.5, 0.0390625, ((0, 64),)),
        "pair_orbitals": draw_pair_orbitals(jax.random.fold_in(key_list[7], 71), 0),
        "orbital_place": draw_orbital_place(jax.random.fold_in(key_list[7], 71), 0),
        "amplitudes": centred(key_list[4], (PAIRS, NPNO * NPNO), 0.2, 3.0, ((0, 256),)),
        "pno_energy": jnp.clip(0.2 + 2.8 * jax.random.uniform(key_list[5], (PAIRS, NPNO), jnp.float32) ** steps_of(key_list[5], (PAIRS, NPNO), ((0, 256),), -0.2, 0.2), 0.2, 3.0),
        "occupied_fock_diagonal": jnp.clip(jax.random.uniform(key_list[6], (NORB,), jnp.float32, -2.0, -0.3), -2.0, -0.3),
    }


def reference(ints_block, pair_vectors, pair_orbitals, orbital_place, amplitudes, pno_energy, occupied_fock_diagonal):
    blocks = PAIRS // PAIR_DEV
    vectors = pair_vectors.reshape(blocks, PAIR_DEV, 2, NPNO, NPAO)
    orbitals = pair_orbitals.reshape(blocks, PAIR_DEV, 2)

    def one_block(args):
        vector_piece, orbs = args
        rows = orbital_place[orbs]
        left_ints = ints_block[rows[:, 0]].astype(jnp.float32)
        left = jnp.einsum("bpa,bxa->bxp", left_ints, vector_piece[:, 0].astype(jnp.float32)).astype(jnp.bfloat16)
        right_ints = ints_block[rows[:, 1]].astype(jnp.float32)
        right = jnp.einsum("bpa,bxa->bxp", right_ints, vector_piece[:, 1].astype(jnp.float32)).astype(jnp.bfloat16)
        exchange = jnp.einsum("bxp,byp->bxy", left.astype(jnp.float32), right.astype(jnp.float32))
        return exchange.reshape(PAIR_DEV, NPNO * NPNO)

    exchange = lax.map(one_block, (vectors, orbitals)).reshape(PAIRS, NPNO * NPNO)
    first = occupied_fock_diagonal[pair_orbitals[:, 0]]
    second = occupied_fock_diagonal[pair_orbitals[:, 1]]
    gap = pno_energy[:, :, None] + pno_energy[:, None, :] - (first + second)[:, None, None]
    return exchange + gap.reshape(PAIRS, NPNO * NPNO) * amplitudes.astype(jnp.float32)
```

```python
import functools

import jax
import jax.numpy as jnp
from jax import lax
from jax.experimental import pallas as pl
from jax.experimental.pallas import tpu as pltpu
from jax.sharding import PartitionSpec as P

CAP = 4
TOGETHER = 8


def route_kernel(keeper, orbitals, place, plane, vectors, sent, slot, row, count, source, sem):
    owners = sent.shape[0]
    entries = vectors.shape[0]

    def clear(o, _):
        count[o] = 0
        source[o] = 0
        for s in range(CAP):
            row[o * CAP + s] = keeper
        return 0

    lax.fori_loop(0, owners, clear, 0)
    mine = plane[0]

    def one(q, _):
        for side in range(2):
            at = place[orbitals[q, side]]
            owner = at // keeper
            position = count[owner]
            count[owner] = position + 1
            slot[q * 2 + side] = position * owners + owner
            row[owner * CAP + position] = at % keeper

            @pl.when(position == mine)
            def _():
                source[owner] = q * 2 + side

        return 0

    lax.fori_loop(0, entries // 2, one, 0)

    def send(o, _):
        pltpu.make_async_copy(vectors.at[source[o]], sent.at[o], sem).start()
        return 0

    lax.fori_loop(0, owners, send, 0)
    pltpu.make_async_copy(vectors.at[pl.ds(0, owners)], sent, sem).wait()


def route(pair_orbitals, orbital_place, plane, vectors, owners, keeper):
    entries, npno, npao = vectors.shape
    smem = pl.BlockSpec(memory_space=pltpu.SMEM)
    return pl.pallas_call(
        functools.partial(route_kernel, keeper),
        out_shape=(
            jax.ShapeDtypeStruct((owners, npno, npao), vectors.dtype),
            jax.ShapeDtypeStruct((entries,), jnp.int32),
            jax.ShapeDtypeStruct((owners * CAP,), jnp.int32),
        ),
        in_specs=[smem, smem, smem, pl.BlockSpec(memory_space=pl.ANY)],
        out_specs=(pl.BlockSpec(memory_space=pl.ANY), smem, smem),
        scratch_shapes=[
            pltpu.SMEM((owners,), jnp.int32),
            pltpu.SMEM((owners,), jnp.int32),
            pltpu.SemaphoreType.DMA,
        ],
        name="route",
    )(pair_orbitals, orbital_place, plane, vectors)


def half_kernel(rows, vectors, ints, out, order, count, stacked):
    keeper = ints.shape[0]
    items, npno, _ = vectors.shape

    for o in range(keeper + 1):
        count[o] = 0

    def sort(e, _):
        o = rows[e]
        n = count[o]
        order[o * items + n] = e
        count[o] = n + 1
        return 0

    lax.fori_loop(0, items, sort, 0)
    stacked[...] = jnp.zeros_like(stacked)
    deep = stacked.shape[1]

    def orbital(o, _):
        n = count[o]

        def block(b, _):
            ids = [
                order[o * items + jnp.minimum(b * TOGETHER + t, n - 1)] for t in range(TOGETHER)
            ]
            for t in range(TOGETHER):
                stacked[t, :npno] = vectors[ids[t]]
            value = jnp.dot(
                stacked[...].reshape(TOGETHER * deep, stacked.shape[2]),
                ints[o],
                preferred_element_type=jnp.float32,
            ).astype(out.dtype)
            for t in range(TOGETHER):
                out[ids[t]] = value[t * deep : t * deep + npno]
            return 0

        lax.fori_loop(0, (n + TOGETHER - 1) // TOGETHER, block, 0)
        return 0

    lax.fori_loop(0, keeper, orbital, 0)


def half(rows, vectors, ints):
    keeper, npao, naux = ints.shape
    items, npno, _ = vectors.shape
    deep = -(-npno // 16) * 16
    vmem = pl.BlockSpec(memory_space=pltpu.VMEM)
    return pl.pallas_call(
        half_kernel,
        out_shape=jax.ShapeDtypeStruct((items, npno, naux), jnp.bfloat16),
        in_specs=[pl.BlockSpec(memory_space=pltpu.SMEM), vmem, vmem],
        out_specs=vmem,
        scratch_shapes=[
            pltpu.SMEM(((keeper + 1) * items,), jnp.int32),
            pltpu.SMEM((keeper + 1,), jnp.int32),
            pltpu.VMEM((TOGETHER, deep, npao), jnp.bfloat16),
        ],
        compiler_params=pltpu.CompilerParams(vmem_limit_bytes=40 * 2**20),
        cost_estimate=pl.CostEstimate(
            flops=2 * items * npno * npao * naux,
            bytes_accessed=2 * (keeper * npao * naux + items * npno * (npao + naux)),
            transcendentals=0,
        ),
        name="half",
    )(rows, vectors, ints)


def exchange_kernel(place, first, second, third, out, halves, sems):
    owners = first.shape[0]
    copies = [
        pltpu.make_async_copy(first, halves.at[pl.ds(0, owners)], sems.at[0]),
        pltpu.make_async_copy(second, halves.at[pl.ds(owners, 2 * owners)], sems.at[1]),
        pltpu.make_async_copy(third, halves.at[pl.ds(3 * owners, owners)], sems.at[2]),
    ]
    for copy in copies:
        copy.start()
    for copy in copies:
        copy.wait()
    group = 8

    def some(g, _):
        for k in range(group):
            q = g * group + k
            out[q] = lax.dot_general(
                halves[place[2 * q]],
                halves[place[2 * q + 1]],
                (((1,), (1,)), ((), ())),
                preferred_element_type=jnp.float32,
            )
        return 0

    lax.fori_loop(0, out.shape[0] // group, some, 0)


def exchange_of(place, first, second, third):
    owners, npno, naux = first.shape
    pairs = place.shape[0] // 2
    return pl.pallas_call(
        exchange_kernel,
        out_shape=jax.ShapeDtypeStruct((pairs, npno, npno), jnp.float32),
        in_specs=[pl.BlockSpec(memory_space=pltpu.SMEM)] + [pl.BlockSpec(memory_space=pl.ANY)] * 3,
        out_specs=pl.BlockSpec(memory_space=pltpu.VMEM),
        scratch_shapes=[
            pltpu.VMEM((CAP * owners, npno, naux), first.dtype),
            pltpu.SemaphoreType.DMA((3,)),
        ],
        compiler_params=pltpu.CompilerParams(vmem_limit_bytes=40 * 2**20),
        name="exchange",
    )(place, first, second, third)


def body(
    ints_block,
    pair_vectors,
    pair_orbitals,
    orbital_place,
    amplitudes,
    pno_energy,
    occupied_fock_diagonal,
):
    n_orb = lax.axis_size("orb")
    n_rep = lax.axis_size("rep")
    orb = lax.axis_index("orb")
    rep = lax.axis_index("rep")
    keeper, naux, npao = ints_block.shape
    pair_dev = pair_vectors.shape[0]
    npno = pair_vectors.shape[2]
    vectors = pair_vectors.reshape(2 * pair_dev, npno, npao)

    sent, slot, row = route(
        pair_orbitals, orbital_place, rep.reshape(1).astype(jnp.int32), vectors, n_orb, keeper
    )
    rows_all = lax.all_gather(row, "orb", axis=0, tiled=False)
    own = lax.all_to_all(sent, "orb", split_axis=0, concat_axis=0, tiled=True)
    ints = jnp.swapaxes(ints_block, 1, 2)
    rows = lax.dynamic_slice_in_dim(rows_all, orb * CAP, CAP, 1)
    rows = jnp.roll(rows, -rep, axis=1).T

    def shifted(value, by):
        return lax.ppermute(value, "rep", [(i, (i + by) % n_rep) for i in range(n_rep)])

    below = shifted(own, 1)
    above = shifted(own, n_rep - 1)
    far_src, below, above = lax.optimization_barrier((own, below, above))
    far = shifted(far_src, 2)

    def back(value):
        return lax.all_to_all(value, "orb", split_axis=0, concat_axis=0, tiled=True)

    half_own = half(rows[0], own, ints)
    first = back(half_own)
    half_above = half(rows[1], above, ints)
    half_below = half(rows[3], below, ints)
    near = jnp.stack([half_above, half_below], axis=1)
    second = back(near)
    third = back(half(rows[2], far, ints))

    position = (slot // n_orb - rep) % n_rep
    owner = slot % n_orb
    place = jnp.where(
        position == 0,
        owner,
        jnp.where(
            position == 2,
            3 * n_orb + owner,
            n_orb + 2 * owner + (position == 3).astype(jnp.int32),
        ),
    )
    partial_value = exchange_of(place, first, second.reshape(2 * n_orb, npno, naux), third)
    mine = pair_dev // n_rep
    partial_value = partial_value.reshape(n_rep, mine, npno * npno)
    parts = lax.all_to_all(partial_value, "rep", split_axis=0, concat_axis=0, tiled=True)
    exchange = jnp.sum(parts, axis=0)
    own_orbs = lax.dynamic_slice_in_dim(pair_orbitals, rep * mine, mine, 0)
    first_fock = occupied_fock_diagonal[own_orbs[:, 0]]
    second_fock = occupied_fock_diagonal[own_orbs[:, 1]]
    gap = pno_energy[:, :, None] + pno_energy[:, None, :] - (first_fock + second_fock)[:, None, None]
    return exchange + gap.reshape(mine, npno * npno) * amplitudes.astype(jnp.float32)


def solution(mesh):
    placed = (
        P("orb", "rep", None),
        P("orb", None, None, None),
        P("orb", None),
        P(),
        P(("orb", "rep"), None),
        P(("orb", "rep"), None),
        P(),
    )
    return jax.shard_map(
        body, mesh=mesh, in_specs=placed, out_specs=P(("orb", "rep"), None), check_vma=False
    )
```

```python
import functools

import jax
import jax.numpy as jnp
from jax import lax
from jax.experimental import pallas as pl
from jax.experimental.pallas import tpu as pltpu
from jax.sharding import PartitionSpec as P

CAP = 4
TOGETHER = 8


LANES = 128
SPARE = 8


def pieces(npno, npao):
    whole = npno // 16 * 16
    blocks = npao // LANES
    cuts = []
    for c in range(blocks):
        lanes = slice(c * LANES, (c + 1) * LANES)
        cuts.append((slice(0, whole), lanes, slice(c * whole, (c + 1) * whole)))
        if npno > whole:
            at = blocks * whole + c * (npno - whole)
            cuts.append((slice(whole, npno), lanes, slice(at, at + npno - whole)))
    return cuts


def route_kernel(
    keeper, orbitals, place, plane, vectors, sent, slot, count, source, row, held, record, sems
):
    owners, npno, npao = held.shape
    pairs = orbitals.shape[1]
    together = 4

    def clear(o, _):
        count[o] = 0
        source[o] = 0
        row[o] = keeper
        return 0

    lax.fori_loop(0, owners, clear, 0, unroll=8)
    mine = plane[0]

    def some(g, _):
        for k in range(together):
            q = g * together + k
            for side in range(2):
                at = place[orbitals[side, q]]
                owner = at // keeper
                position = count[owner]
                count[owner] = position + 1
                slot[q * 2 + side] = position * owners + owner
                to = owner + jnp.where(position == mine, 0, owners)
                source[to] = q * 2 + side
                row[to] = at % keeper
        return 0

    lax.fori_loop(0, pairs // together, some, 0)

    def fetch(o, _):
        pltpu.make_async_copy(vectors.at[source[o]], held.at[o], sems.at[0]).start()
        return 0

    lax.fori_loop(0, owners, fetch, 0, unroll=8)
    pltpu.make_async_copy(vectors.at[pl.ds(0, owners)], held, sems.at[0]).wait()

    def lay(o, _):
        for rows, lanes, at in pieces(npno, npao):
            record[o, at, :] = held[o, rows, lanes]
        number = jnp.full((SPARE, LANES), row[o], jnp.int32).astype(jnp.float32)
        record[o, npno * npao // LANES :, :] = number.astype(record.dtype)
        return 0

    lax.fori_loop(0, owners, lay, 0, unroll=2)
    out = pltpu.make_async_copy(record, sent, sems.at[1])
    out.start()
    out.wait()


def route(orbitals, orbital_place, plane, vectors, owners, keeper):
    entries, npno, npao = vectors.shape
    depth = npno * npao // LANES + SPARE
    smem = pl.BlockSpec(memory_space=pltpu.SMEM)
    hbm = pl.BlockSpec(memory_space=pltpu.HBM)
    return pl.pallas_call(
        functools.partial(route_kernel, keeper),
        out_shape=(
            jax.ShapeDtypeStruct((owners, depth, LANES), vectors.dtype),
            jax.ShapeDtypeStruct((entries,), jnp.int32),
        ),
        in_specs=[smem, smem, smem, hbm],
        out_specs=(hbm, smem),
        scratch_shapes=[
            pltpu.SMEM((owners,), jnp.int32),
            pltpu.SMEM((2 * owners,), jnp.int32),
            pltpu.SMEM((2 * owners,), jnp.int32),
            pltpu.VMEM((owners, npno, npao), vectors.dtype),
            pltpu.VMEM((owners, depth, LANES), vectors.dtype),
            pltpu.SemaphoreType.DMA((2,)),
        ],
        compiler_params=pltpu.CompilerParams(vmem_limit_bytes=60 * 2**20),
        name="route",
    )(orbitals, orbital_place, plane, vectors)


def half_kernel(parts, npno, *refs):
    rows, records, (ints, out) = refs[:parts], refs[parts : 2 * parts], refs[2 * parts : 2 * parts + 2]
    order, count, stacked, vectors, blocks, halves, sems = refs[2 * parts + 2 :]
    keeper, npao, _ = ints.shape
    items = records[0].shape[0]
    deep = stacked.shape[1]
    copies = [
        pltpu.make_async_copy(records[part], vectors.at[part], sems.at[keeper + part])
        for part in range(parts)
    ]
    loads = [pltpu.make_async_copy(ints.at[o], blocks.at[o], sems.at[o]) for o in range(keeper)]
    copies[0].start()
    for load in loads:
        load.start()
    for copy in copies[1:]:
        copy.start()
    stacked[...] = jnp.zeros_like(stacked)

    for part in range(parts):
        for o in range(keeper + 1):
            count[o] = 0

        def sort(e, _):
            o = rows[part][e]
            n = count[o]
            order[o * items + n] = e
            count[o] = n + 1
            return 0

        lax.fori_loop(0, items, sort, 0, unroll=8)
        copies[part].wait()

        for o in range(keeper):
            if part == 0:
                loads[o].wait()
            n = count[o]

            def block(b, _):
                ids = [
                    order[o * items + jnp.minimum(b * TOGETHER + t, n - 1)]
                    for t in range(TOGETHER)
                ]
                for t in range(TOGETHER):
                    for held, lanes, at in pieces(npno, npao):
                        stacked[t, held, lanes] = vectors[part, ids[t], at, :]
                value = jnp.dot(
                    stacked[...].reshape(TOGETHER * deep, npao),
                    blocks[o],
                    preferred_element_type=jnp.float32,
                ).astype(out.dtype)
                for t in range(TOGETHER):
                    halves[ids[t], part] = value[t * deep : t * deep + npno]
                return 0

            lax.fori_loop(0, (n + TOGETHER - 1) // TOGETHER, block, 0)

    back = pltpu.make_async_copy(halves, out, sems.at[keeper + parts])
    back.start()
    back.wait()


def half(rows, records, ints, npno):
    parts = len(records)
    keeper, npao, naux = ints.shape
    items, depth, _ = records[0].shape
    deep = -(-npno // 16) * 16
    hbm = pl.BlockSpec(memory_space=pltpu.HBM)
    return pl.pallas_call(
        functools.partial(half_kernel, parts, npno),
        out_shape=jax.ShapeDtypeStruct((items, parts, npno, naux), jnp.bfloat16),
        in_specs=[pl.BlockSpec(memory_space=pltpu.SMEM)] * parts + [hbm] * (parts + 1),
        out_specs=hbm,
        scratch_shapes=[
            pltpu.SMEM(((keeper + 1) * items,), jnp.int32),
            pltpu.SMEM((keeper + 1,), jnp.int32),
            pltpu.VMEM((TOGETHER, deep, npao), jnp.bfloat16),
            pltpu.VMEM((parts, items, depth, LANES), jnp.bfloat16),
            pltpu.VMEM((keeper, npao, naux), jnp.bfloat16),
            pltpu.VMEM((items, parts, npno, naux), jnp.bfloat16),
            pltpu.SemaphoreType.DMA((keeper + parts + 1,)),
        ],
        compiler_params=pltpu.CompilerParams(vmem_limit_bytes=60 * 2**20),
        cost_estimate=pl.CostEstimate(
            flops=16 * parts * items * npno * npao * naux,
            bytes_accessed=2 * (keeper * npao * naux + parts * items * npno * (npao + naux)),
            transcendentals=0,
        ),
        name="half",
    )(*rows, *records, ints)


def exchange_kernel(place, first, second, third, out, halves, sems):
    owners = first.shape[0]
    copies = [
        pltpu.make_async_copy(first, halves.at[pl.ds(0, owners)], sems.at[0]),
        pltpu.make_async_copy(second, halves.at[pl.ds(owners, 2 * owners)], sems.at[1]),
        pltpu.make_async_copy(third, halves.at[pl.ds(3 * owners, owners)], sems.at[2]),
    ]
    for copy in copies:
        copy.start()
    for copy in copies:
        copy.wait()
    group = 8

    def some(g, _):
        for k in range(group):
            q = g * group + k
            out[q] = lax.dot_general(
                halves[place[2 * q]],
                halves[place[2 * q + 1]],
                (((1,), (1,)), ((), ())),
                preferred_element_type=jnp.float32,
            )
        return 0

    lax.fori_loop(0, out.shape[0] // group, some, 0)


def exchange_of(place, first, second, third):
    owners, npno, naux = first.shape
    pairs = place.shape[0] // 2
    return pl.pallas_call(
        exchange_kernel,
        out_shape=jax.ShapeDtypeStruct((pairs, npno, npno), jnp.float32),
        in_specs=[pl.BlockSpec(memory_space=pltpu.SMEM)] + [pl.BlockSpec(memory_space=pltpu.HBM)] * 3,
        out_specs=pl.BlockSpec(memory_space=pltpu.VMEM),
        scratch_shapes=[
            pltpu.VMEM((CAP * owners, npno, naux), first.dtype),
            pltpu.SemaphoreType.DMA((3,)),
        ],
        compiler_params=pltpu.CompilerParams(vmem_limit_bytes=60 * 2**20),
        name="exchange",
    )(place, first, second, third)


def body(
    ints_block,
    pair_vectors,
    pair_orbitals,
    orbital_place,
    amplitudes,
    pno_energy,
    occupied_fock_diagonal,
):
    n_orb = lax.axis_size("orb")
    n_rep = lax.axis_size("rep")
    rep = lax.axis_index("rep")
    keeper, naux, npao = ints_block.shape
    pair_dev = pair_vectors.shape[0]
    npno = pair_vectors.shape[2]
    vectors = pair_vectors.reshape(2 * pair_dev, npno, npao)

    def shifted(value, by):
        return lax.ppermute(value, "rep", [(i, (i + by) % n_rep) for i in range(n_rep)])

    def there(value):
        return lax.all_to_all(value, "orb", split_axis=0, concat_axis=0, tiled=True)

    def row_of(record):
        return record[:, npno * npao // LANES, 0].astype(jnp.int32)

    def halves(*records):
        return half(tuple(row_of(record) for record in records), records, ints, npno)

    sent, slot = route(
        pair_orbitals.T, orbital_place, rep.reshape(1).astype(jnp.int32), vectors, n_orb, keeper
    )
    own = there(sent)
    ints = jnp.swapaxes(lax.optimization_barrier((ints_block, sent))[0], 1, 2)
    own, ints = lax.optimization_barrier((own, ints))
    below = shifted(own, 1)
    above = shifted(own, n_rep - 1)
    first = there(halves(own))
    near = halves(above, below)
    near, first = lax.optimization_barrier((near, first))
    second = there(near)
    far = halves(shifted(lax.optimization_barrier((own, below, above))[0], 2))
    far, second = lax.optimization_barrier((far, second))
    third = there(far)

    position = (slot // n_orb - rep) % n_rep
    owner = slot % n_orb
    place = jnp.where(
        position == 0,
        owner,
        jnp.where(
            position == 2,
            3 * n_orb + owner,
            n_orb + 2 * owner + (position == 3).astype(jnp.int32),
        ),
    )
    partial_value = exchange_of(
        place, *(part.reshape(-1, npno, naux) for part in (first, second, third))
    )
    mine = pair_dev // n_rep
    partial_value = partial_value.reshape(n_rep, mine, npno * npno)
    exchange = lax.dynamic_index_in_dim(partial_value, rep, 0, keepdims=False)
    for by in (1, n_rep - 1, 2):
        leaving = lax.dynamic_index_in_dim(partial_value, (rep + by) % n_rep, 0, keepdims=False)
        exchange = exchange + shifted(leaving, by)
    own_orbs = lax.dynamic_slice_in_dim(pair_orbitals, rep * mine, mine, 0)
    first_fock = occupied_fock_diagonal[own_orbs[:, 0]]
    second_fock = occupied_fock_diagonal[own_orbs[:, 1]]
    gap = pno_energy[:, :, None] + pno_energy[:, None, :] - (first_fock + second_fock)[:, None, None]
    return exchange + gap.reshape(mine, npno * npno) * amplitudes.astype(jnp.float32)


def solution(mesh):
    placed = (
        P("orb", "rep", None),
        P("orb", None, None, None),
        P("orb", None),
        P(),
        P(("orb", "rep"), None),
        P(("orb", "rep"), None),
        P(),
    )
    return jax.shard_map(
        body, mesh=mesh, in_specs=placed, out_specs=P(("orb", "rep"), None), check_vma=False
    )
```

```python
import functools

import jax
import jax.numpy as jnp
from jax import lax
from jax.experimental import pallas as pl
from jax.experimental.pallas import tpu as pltpu
from jax.sharding import PartitionSpec as P

CAP = 4
TOGETHER = 8
WEIGHT = 8


LANES = 128
SPARE = 8


def pieces(npno, npao):
    whole = npno // 16 * 16
    blocks = npao // LANES
    cuts = []
    for c in range(blocks):
        lanes = slice(c * LANES, (c + 1) * LANES)
        cuts.append((slice(0, whole), lanes, slice(c * whole, (c + 1) * whole)))
        if npno > whole:
            at = blocks * whole + c * (npno - whole)
            cuts.append((slice(whole, npno), lanes, slice(at, at + npno - whole)))
    return cuts


def route_kernel(
    keeper, orbitals, place, plane, vectors, sent, slot, count, source, row, held, record, sems
):
    owners, npno, npao = held.shape
    pairs = orbitals.shape[1]
    together = 4

    def clear(o, _):
        count[o] = 0
        source[o] = 0
        row[o] = keeper
        return 0

    lax.fori_loop(0, owners, clear, 0, unroll=8)
    mine = plane[0]

    def some(g, _):
        for k in range(together):
            q = g * together + k
            for side in range(2):
                at = place[orbitals[side, q]]
                owner = at // keeper
                position = count[owner]
                count[owner] = position + 1
                slot[q * 2 + side] = position * owners + owner
                to = owner + jnp.where(position == mine, 0, owners)
                source[to] = q * 2 + side
                row[to] = at % keeper
        return 0

    lax.fori_loop(0, pairs // together, some, 0)

    def fetch(o, _):
        pltpu.make_async_copy(vectors.at[source[o]], held.at[o], sems.at[0]).start()
        return 0

    lax.fori_loop(0, owners, fetch, 0, unroll=8)
    pltpu.make_async_copy(vectors.at[pl.ds(0, owners)], held, sems.at[0]).wait()

    def lay(o, _):
        for rows, lanes, at in pieces(npno, npao):
            record[o, at, :] = held[o, rows, lanes]
        number = jnp.full((SPARE, LANES), row[o], jnp.int32).astype(jnp.float32)
        record[o, npno * npao // LANES :, :] = number.astype(record.dtype)
        return 0

    lax.fori_loop(0, owners, lay, 0, unroll=2)
    out = pltpu.make_async_copy(record, sent, sems.at[1])
    out.start()
    out.wait()


def route(orbitals, orbital_place, plane, vectors, owners, keeper):
    entries, npno, npao = vectors.shape
    depth = npno * npao // LANES + SPARE
    smem = pl.BlockSpec(memory_space=pltpu.SMEM)
    hbm = pl.BlockSpec(memory_space=pltpu.HBM)
    return pl.pallas_call(
        functools.partial(route_kernel, keeper),
        out_shape=(
            jax.ShapeDtypeStruct((owners, depth, LANES), vectors.dtype),
            jax.ShapeDtypeStruct((entries,), jnp.int32),
        ),
        in_specs=[smem, smem, smem, hbm],
        out_specs=(hbm, smem),
        scratch_shapes=[
            pltpu.SMEM((owners,), jnp.int32),
            pltpu.SMEM((2 * owners,), jnp.int32),
            pltpu.SMEM((2 * owners,), jnp.int32),
            pltpu.VMEM((owners, npno, npao), vectors.dtype),
            pltpu.VMEM((owners, depth, LANES), vectors.dtype),
            pltpu.SemaphoreType.DMA((2,)),
        ],
        compiler_params=pltpu.CompilerParams(vmem_limit_bytes=60 * 2**20),
        name="route",
    )(orbitals, orbital_place, plane, vectors)


def half_kernel(shares, record, *refs):
    ints, out = refs[:shares], refs[shares]
    held, order, count, number, row, stacked, blocks, halves, sems = refs[shares + 1 :]
    items, _, npno, naux = out.shape
    keeper, _, npao = blocks.shape
    deep = stacked.shape[1]
    whole = pltpu.make_async_copy(record, held, sems.at[0])
    whole.start()
    loads = [
        pltpu.make_async_copy(
            ints[k].at[o], blocks.at[o, pl.ds(k * naux, naux)], sems.at[2 + shares + o * shares + k]
        )
        for o in range(keeper)
        for k in range(shares)
    ]
    for load in loads:
        load.start()
    stacked[...] = jnp.zeros_like(stacked)
    whole.wait()

    tile = held[:, npno * npao // LANES :, :].astype(jnp.float32)
    own = lax.broadcasted_iota(jnp.int32, tile.shape, 0)
    lane = lax.broadcasted_iota(jnp.int32, tile.shape, 2)
    number[...] = jnp.sum(jnp.where(own == lane, tile, 0.0), axis=0).astype(jnp.int32)
    move = pltpu.make_async_copy(number, row, sems.at[1])
    move.start()
    move.wait()
    for o in range(keeper + 1):
        count[o] = 0

    def sort(e, _):
        o = row[0, e]
        n = count[o]
        order[o * items + n] = e
        count[o] = n + 1
        return 0

    lax.fori_loop(0, items, sort, 0, unroll=8)

    for o in range(keeper):
        for k in range(shares):
            loads[o * shares + k].wait()
        n = count[o]

        def block(b, _):
            ids = [
                order[o * items + jnp.minimum(b * TOGETHER + t, n - 1)] for t in range(TOGETHER)
            ]
            for t in range(TOGETHER):
                for rows, lanes, at in pieces(npno, npao):
                    stacked[t, rows, lanes] = held[ids[t], at, :]
            value = lax.dot_general(
                stacked[...].reshape(TOGETHER * deep, npao),
                blocks[o],
                (((1,), (1,)), ((), ())),
                preferred_element_type=jnp.float32,
            ).astype(out.dtype)
            for t in range(TOGETHER):
                for k in range(shares):
                    halves[k, ids[t]] = value[
                        t * deep : t * deep + npno, k * naux : (k + 1) * naux
                    ]
            return 0

        lax.fori_loop(0, (n + TOGETHER - 1) // TOGETHER, block, 0)

    backs = [
        pltpu.make_async_copy(halves.at[k], out.at[:, k], sems.at[2 + k]) for k in range(shares)
    ]
    for back in backs:
        back.start()
    for back in backs:
        back.wait()


def half(record, ints, npno, weight):
    shares = len(ints)
    keeper, naux, npao = ints[0].shape
    items = record.shape[0]
    hbm = pl.BlockSpec(memory_space=pltpu.HBM)
    return pl.pallas_call(
        functools.partial(half_kernel, shares),
        out_shape=jax.ShapeDtypeStruct((items, shares, npno, naux), jnp.bfloat16),
        in_specs=[hbm] * (1 + shares),
        out_specs=hbm,
        scratch_shapes=[
            pltpu.VMEM(record.shape, record.dtype),
            pltpu.SMEM(((keeper + 1) * items,), jnp.int32),
            pltpu.SMEM((keeper + 1,), jnp.int32),
            pltpu.VMEM((SPARE, LANES), jnp.int32),
            pltpu.SMEM((SPARE, LANES), jnp.int32),
            pltpu.VMEM((TOGETHER, -(-npno // 16) * 16, npao), jnp.bfloat16),
            pltpu.VMEM((keeper, shares * naux, npao), jnp.bfloat16),
            pltpu.VMEM((shares, items, npno, naux), jnp.bfloat16),
            pltpu.SemaphoreType.DMA((2 + shares + keeper * shares,)),
        ],
        compiler_params=pltpu.CompilerParams(vmem_limit_bytes=60 * 2**20),
        cost_estimate=pl.CostEstimate(
            flops=weight * 2 * shares * items * npno * npao * naux,
            bytes_accessed=2 * shares * (keeper * npao * naux + items * npno * (npao + naux)),
            transcendentals=0,
        ),
        name="half",
    )(record, *ints)


def exchange_kernel(place, *refs):
    out, halves, sems = refs[CAP:]
    owners = refs[0].shape[0]
    copies = [
        pltpu.make_async_copy(refs[k], halves.at[pl.ds(k * owners, owners)], sems.at[k])
        for k in range(CAP)
    ]
    for copy in copies:
        copy.start()
    for copy in copies:
        copy.wait()
    group = 16

    def some(g, _):
        for k in range(group):
            q = g * group + k
            out[q] = lax.dot_general(
                halves[place[2 * q]],
                halves[place[2 * q + 1]],
                (((1,), (1,)), ((), ())),
                preferred_element_type=jnp.float32,
            )
        return 0

    lax.fori_loop(0, out.shape[0] // group, some, 0)


def exchange_of(place, parts):
    owners, npno, naux = parts[0].shape
    pairs = place.shape[0] // 2
    hbm = pl.BlockSpec(memory_space=pltpu.HBM)
    return pl.pallas_call(
        exchange_kernel,
        out_shape=jax.ShapeDtypeStruct((pairs, npno, npno), jnp.float32),
        in_specs=[pl.BlockSpec(memory_space=pltpu.SMEM)] + [hbm] * CAP,
        out_specs=pl.BlockSpec(memory_space=pltpu.VMEM),
        scratch_shapes=[
            pltpu.VMEM((CAP * owners, npno, naux), jnp.bfloat16),
            pltpu.SemaphoreType.DMA((CAP,)),
        ],
        compiler_params=pltpu.CompilerParams(vmem_limit_bytes=60 * 2**20),
        name="exchange",
    )(place, *parts)


def body(
    ints_block,
    pair_vectors,
    pair_orbitals,
    orbital_place,
    amplitudes,
    pno_energy,
    occupied_fock_diagonal,
):
    n_orb = lax.axis_size("orb")
    n_rep = lax.axis_size("rep")
    rep = lax.axis_index("rep")
    keeper, naux, npao = ints_block.shape
    pair_dev = pair_vectors.shape[0]
    npno = pair_vectors.shape[2]
    vectors = pair_vectors.reshape(2 * pair_dev, npno, npao)

    def shifted(value, by):
        return lax.ppermute(value, "rep", [(i, (i + by) % n_rep) for i in range(n_rep)])

    def there(value):
        return lax.all_to_all(value, "orb", split_axis=0, concat_axis=0, tiled=True)

    sent, slot = route(
        pair_orbitals.T, orbital_place, rep.reshape(1).astype(jnp.int32), vectors, n_orb, keeper
    )
    own = there(sent)

    above = shifted(ints_block, n_rep - 1)
    below = shifted(ints_block, 1)
    opposite = shifted(own, 2)

    first = there(half(own, (ints_block,), npno, WEIGHT))
    near, first = lax.optimization_barrier((half(own, (above, below), npno, WEIGHT), first))
    near = there(near)
    far, near = lax.optimization_barrier((half(opposite, (ints_block,), npno, WEIGHT), near))
    far = there(far)

    parts = (
        first[:, 0],
        shifted(near[:, 1], n_rep - 1),
        far[:, 0],
        shifted(near[:, 0], 1),
    )
    place = (slot // n_orb - rep) % n_rep * n_orb + slot % n_orb
    partial_value = exchange_of(place, parts)
    mine = pair_dev // n_rep
    partial_value = partial_value.reshape(n_rep, mine, npno * npno)
    exchange = lax.dynamic_index_in_dim(partial_value, rep, 0, keepdims=False)
    for by in (1, n_rep - 1, 2):
        leaving = lax.dynamic_index_in_dim(partial_value, (rep + by) % n_rep, 0, keepdims=False)
        exchange = exchange + shifted(leaving, by)
    own_orbs = lax.dynamic_slice_in_dim(pair_orbitals, rep * mine, mine, 0)
    first_fock = occupied_fock_diagonal[own_orbs[:, 0]]
    second_fock = occupied_fock_diagonal[own_orbs[:, 1]]
    gap = pno_energy[:, :, None] + pno_energy[:, None, :] - (first_fock + second_fock)[:, None, None]
    return exchange + gap.reshape(mine, npno * npno) * amplitudes.astype(jnp.float32)


def solution(mesh):
    placed = (
        P("orb", "rep", None),
        P("orb", None, None, None),
        P("orb", None),
        P(),
        P(("orb", "rep"), None),
        P(("orb", "rep"), None),
        P(),
    )
    return jax.shard_map(
        body, mesh=mesh, in_specs=placed, out_specs=P(("orb", "rep"), None), check_vma=False
    )
```

```python
import functools

import jax
import jax.numpy as jnp
from jax import lax
from jax.experimental import pallas as pl
from jax.experimental.pallas import tpu as pltpu
from jax.sharding import PartitionSpec as P

CAP = 4
TOGETHER = 8


LANES = 128
SPARE = 8


def pieces(npno, npao):
    whole = npno // 16 * 16
    blocks = npao // LANES
    cuts = []
    for c in range(blocks):
        lanes = slice(c * LANES, (c + 1) * LANES)
        cuts.append((slice(0, whole), lanes, slice(c * whole, (c + 1) * whole)))
        if npno > whole:
            at = blocks * whole + c * (npno - whole)
            cuts.append((slice(whole, npno), lanes, slice(at, at + npno - whole)))
    return cuts


def route_kernel(
    keeper, orbitals, place, plane, vectors, sent, slot, count, source, row, held, record, sems
):
    owners, npno, npao = held.shape
    pairs = orbitals.shape[1]
    together = 4

    def clear(o, _):
        count[o] = 0
        source[o] = 0
        row[o] = keeper
        return 0

    lax.fori_loop(0, owners, clear, 0, unroll=8)
    mine = plane[0]

    def some(g, _):
        for k in range(together):
            q = g * together + k
            for side in range(2):
                at = place[orbitals[side, q]]
                owner = at // keeper
                position = count[owner]
                count[owner] = position + 1
                slot[q * 2 + side] = position * owners + owner
                to = owner + jnp.where(position == mine, 0, owners)
                source[to] = q * 2 + side
                row[to] = at % keeper
        return 0

    lax.fori_loop(0, pairs // together, some, 0)

    def fetch(o, _):
        pltpu.make_async_copy(vectors.at[source[o]], held.at[o], sems.at[0]).start()
        return 0

    lax.fori_loop(0, owners, fetch, 0, unroll=8)
    pltpu.make_async_copy(vectors.at[pl.ds(0, owners)], held, sems.at[0]).wait()

    def lay(o, _):
        for rows, lanes, at in pieces(npno, npao):
            record[o, at, :] = held[o, rows, lanes]
        number = jnp.full((SPARE, LANES), row[o], jnp.int32).astype(jnp.float32)
        record[o, npno * npao // LANES :, :] = number.astype(record.dtype)
        return 0

    lax.fori_loop(0, owners, lay, 0, unroll=2)
    out = pltpu.make_async_copy(record, sent, sems.at[1])
    out.start()
    out.wait()


def route(orbitals, orbital_place, plane, vectors, owners, keeper):
    entries, npno, npao = vectors.shape
    depth = npno * npao // LANES + SPARE
    smem = pl.BlockSpec(memory_space=pltpu.SMEM)
    hbm = pl.BlockSpec(memory_space=pltpu.HBM)
    return pl.pallas_call(
        functools.partial(route_kernel, keeper),
        out_shape=(
            jax.ShapeDtypeStruct((owners, depth, LANES), vectors.dtype),
            jax.ShapeDtypeStruct((entries,), jnp.int32),
        ),
        in_specs=[smem, smem, smem, hbm],
        out_specs=(hbm, smem),
        scratch_shapes=[
            pltpu.SMEM((owners,), jnp.int32),
            pltpu.SMEM((2 * owners,), jnp.int32),
            pltpu.SMEM((2 * owners,), jnp.int32),
            pltpu.VMEM((owners, npno, npao), vectors.dtype),
            pltpu.VMEM((owners, depth, LANES), vectors.dtype),
            pltpu.SemaphoreType.DMA((2,)),
        ],
        compiler_params=pltpu.CompilerParams(vmem_limit_bytes=60 * 2**20),
        name="route",
    )(orbitals, orbital_place, plane, vectors)


def sort_entries(held, number, row, count, order, sem, keeper, at):
    items = held.shape[0]
    tile = held[:, at:, :].astype(jnp.float32)
    own = lax.broadcasted_iota(jnp.int32, tile.shape, 0)
    lane = lax.broadcasted_iota(jnp.int32, tile.shape, 2)
    number[...] = jnp.sum(jnp.where(own == lane, tile, 0.0), axis=0).astype(jnp.int32)
    move = pltpu.make_async_copy(number, row, sem)
    move.start()
    move.wait()
    for o in range(keeper + 1):
        count[o] = 0

    def sort(e, _):
        o = row[0, e]
        n = count[o]
        order[o * items + n] = e
        count[o] = n + 1
        return 0

    lax.fori_loop(0, items, sort, 0, unroll=8)


def stack(stacked, held, ids, npno):
    npao = stacked.shape[2]
    for t, e in enumerate(ids):
        for rows, lanes, at in pieces(npno, npao):
            stacked[t, rows, lanes] = held[e, at, :]
    return stacked[...].reshape(-1, npao)


def near_kernel(
    npno, record, own, above, below, out, rest_out,
    held, order, count, number, row, stacked, blocks, halves, rest, sems,
):
    keeper, naux, npao = own.shape
    items, tail, _ = rest.shape
    main = npno - tail
    deep = stacked.shape[1]
    whole = pltpu.make_async_copy(record, held, sems.at[0])
    whole.start()
    loads = [
        pltpu.make_async_copy(
            share.at[o], blocks.at[o, pl.ds(k * naux, naux)], sems.at[4 + 3 * o + k]
        )
        for o in range(keeper)
        for k, share in enumerate((own, above, below))
    ]
    for load in loads:
        load.start()
    stacked[...] = jnp.zeros_like(stacked)
    whole.wait()
    sort_entries(held, number, row, count, order, sems.at[1], keeper, npno * npao // LANES)

    def goes(e):
        return pltpu.make_async_copy(halves.at[e], out.at[e], sems.at[2])

    for o in range(keeper):
        for k in range(3):
            loads[3 * o + k].wait()
        n = count[o]

        def block(b, _):
            at = [b * TOGETHER + t for t in range(TOGETHER)]
            ids = [order[o * items + jnp.minimum(k, n - 1)] for k in at]
            value = lax.dot_general(
                stack(stacked, held, ids, npno),
                blocks[o],
                (((1,), (1,)), ((), ())),
                preferred_element_type=jnp.float32,
            ).astype(out.dtype)
            for t, e in enumerate(ids):
                rows = value[t * deep : t * deep + npno]
                halves[e, :main] = rows[:main, :naux]
                rest[e] = rows[main:, :naux]
                halves[e, main : main + npno] = rows[:, naux : 2 * naux]
                halves[e, main + npno :] = rows[:, 2 * naux :]
            for k, e in zip(at, ids):

                @pl.when(k < n)
                def _():
                    goes(e).start()

            return 0

        lax.fori_loop(0, (n + TOGETHER - 1) // TOGETHER, block, 0)

    back = pltpu.make_async_copy(rest, rest_out, sems.at[3])
    back.start()

    def arrive(e, _):
        goes(0).wait()
        return 0

    lax.fori_loop(0, items - count[keeper], arrive, 0)
    back.wait()


def near_halves(record, own, above, below, npno):
    keeper, naux, npao = own.shape
    items = record.shape[0]
    tail = npno % 16
    rows = 3 * npno - tail
    hbm = pl.BlockSpec(memory_space=pltpu.HBM)
    return pl.pallas_call(
        functools.partial(near_kernel, npno),
        out_shape=[
            jax.ShapeDtypeStruct((items, rows, naux), jnp.bfloat16),
            jax.ShapeDtypeStruct((items, tail, naux), jnp.bfloat16),
        ],
        in_specs=[hbm] * 4,
        out_specs=[hbm] * 2,
        scratch_shapes=[
            pltpu.VMEM(record.shape, record.dtype),
            pltpu.SMEM(((keeper + 1) * items,), jnp.int32),
            pltpu.SMEM((keeper + 1,), jnp.int32),
            pltpu.VMEM((SPARE, LANES), jnp.int32),
            pltpu.SMEM((SPARE, LANES), jnp.int32),
            pltpu.VMEM((TOGETHER, -(-npno // 16) * 16, npao), jnp.bfloat16),
            pltpu.VMEM((keeper, 3 * naux, npao), jnp.bfloat16),
            pltpu.VMEM((items, rows, naux), jnp.bfloat16),
            pltpu.VMEM((items, tail, naux), jnp.bfloat16),
            pltpu.SemaphoreType.DMA((4 + 3 * keeper,)),
        ],
        compiler_params=pltpu.CompilerParams(vmem_limit_bytes=60 * 2**20),
        cost_estimate=pl.CostEstimate(
            flops=6 * items * npno * npao * naux,
            bytes_accessed=2 * (3 * keeper * npao * naux + items * npno * (npao + 3 * naux)),
            transcendentals=0,
        ),
        name="near",
    )(record, own, above, below)


def far_kernel(npno, record, ints, rest_in, out, held, order, count, number, row, stacked, blocks, halves, rest, sems):
    keeper, naux, npao = ints.shape
    items = held.shape[0]
    deep = stacked.shape[1]
    whole = pltpu.make_async_copy(record, held, sems.at[0])
    load = pltpu.make_async_copy(ints, blocks, sems.at[1])
    rest_load = pltpu.make_async_copy(rest_in, rest, sems.at[2])
    for copy in (whole, load, rest_load):
        copy.start()
    stacked[...] = jnp.zeros_like(stacked)
    whole.wait()
    sort_entries(held, number, row, count, order, sems.at[3], keeper, npno * npao // LANES)
    load.wait()
    for o in range(keeper):
        n = count[o]

        def block(b, _):
            ids = [
                order[o * items + jnp.minimum(b * TOGETHER + t, n - 1)] for t in range(TOGETHER)
            ]
            value = lax.dot_general(
                stack(stacked, held, ids, npno),
                blocks[o],
                (((1,), (1,)), ((), ())),
                preferred_element_type=jnp.float32,
            ).astype(out.dtype)
            for t, e in enumerate(ids):
                halves[e, :npno] = value[t * deep : t * deep + npno]
            return 0

        lax.fori_loop(0, (n + TOGETHER - 1) // TOGETHER, block, 0)

    rest_load.wait()

    def join(e, _):
        halves[e, npno:] = rest[e]
        return 0

    lax.fori_loop(0, items, join, 0, unroll=8)
    back = pltpu.make_async_copy(halves, out, sems.at[4])
    back.start()
    back.wait()


def far_halves(record, ints, rest, npno):
    keeper, naux, npao = ints.shape
    items, tail, _ = rest.shape
    hbm = pl.BlockSpec(memory_space=pltpu.HBM)
    return pl.pallas_call(
        functools.partial(far_kernel, npno),
        out_shape=jax.ShapeDtypeStruct((items, npno + tail, naux), jnp.bfloat16),
        in_specs=[hbm] * 3,
        out_specs=hbm,
        scratch_shapes=[
            pltpu.VMEM(record.shape, record.dtype),
            pltpu.SMEM(((keeper + 1) * items,), jnp.int32),
            pltpu.SMEM((keeper + 1,), jnp.int32),
            pltpu.VMEM((SPARE, LANES), jnp.int32),
            pltpu.SMEM((SPARE, LANES), jnp.int32),
            pltpu.VMEM((TOGETHER, -(-npno // 16) * 16, npao), jnp.bfloat16),
            pltpu.VMEM(ints.shape, jnp.bfloat16),
            pltpu.VMEM((items, npno + tail, naux), jnp.bfloat16),
            pltpu.VMEM(rest.shape, jnp.bfloat16),
            pltpu.SemaphoreType.DMA((5,)),
        ],
        compiler_params=pltpu.CompilerParams(vmem_limit_bytes=60 * 2**20),
        cost_estimate=pl.CostEstimate(
            flops=16 * items * npno * npao * naux,
            bytes_accessed=2 * (keeper * npao * naux + items * npno * (npao + naux)),
            transcendentals=0,
        ),
        name="far",
    )(record, ints, rest)


def hold_kernel(above_in, below_in, above, below):
    pass


def hold(above, below):
    hbm = pl.BlockSpec(memory_space=pltpu.HBM)
    return pl.pallas_call(
        hold_kernel,
        out_shape=[jax.ShapeDtypeStruct(above.shape, above.dtype)] * 2,
        in_specs=[hbm] * 2,
        out_specs=[hbm] * 2,
        input_output_aliases={0: 0, 1: 1},
        compiler_params=pltpu.CompilerParams(vmem_limit_bytes=60 * 2**20),
        cost_estimate=pl.CostEstimate(flops=10**11, bytes_accessed=0, transcendentals=0),
        name="hold",
    )(above, below)


def exchange_kernel(place, first, above, last, below, *refs):
    planes = len(refs) - 4
    outs, (halves, late, product, sems) = refs[:planes], refs[planes:]
    owners, main, _ = first.shape
    npno = halves.shape[1]
    copies = [
        pltpu.make_async_copy(last, late, sems.at[0]),
        pltpu.make_async_copy(
            first, halves.at[pl.ds(0, owners), pl.ds(0, main)], sems.at[1]
        ),
        pltpu.make_async_copy(above, halves.at[pl.ds(owners, owners)], sems.at[2]),
        pltpu.make_async_copy(below, halves.at[pl.ds(3 * owners, owners)], sems.at[3]),
    ]
    for copy in copies:
        copy.start()
    copies[0].wait()

    def join(e, _):
        halves[e, main:] = late[e, npno:]
        halves[2 * owners + e] = late[e, :npno]
        return 0

    lax.fori_loop(0, owners, join, 0, unroll=4)
    for copy in copies[1:]:
        copy.wait()
    each = outs[0].shape[0]

    def some(g, _):
        for k in range(each):
            q = g * each + k
            at = pl.multiple_of(q * npno, 8)
            product[pl.ds(at, npno), :npno] = lax.dot_general(
                halves[place[2 * q]],
                halves[place[2 * q + 1]],
                (((1,), (1,)), ((), ())),
                preferred_element_type=jnp.float32,
            )
        return 0

    lax.fori_loop(0, planes, some, 0)
    for g in range(planes):
        for x in range(npno):
            rows = product[pl.ds(g * each * npno + x, each, stride=npno), :]
            outs[g][:, x * npno : (x + 1) * npno] = rows[:, :npno]


def exchange_of(place, planes, first, above, last, below):
    owners, npno, naux = above.shape
    pairs = place.shape[0] // 2
    hbm = pl.BlockSpec(memory_space=pltpu.HBM)
    vmem = pl.BlockSpec(memory_space=pltpu.VMEM)
    out = jax.ShapeDtypeStruct((pairs // planes, npno * npno), jnp.float32)
    return pl.pallas_call(
        exchange_kernel,
        out_shape=[out] * planes,
        in_specs=[pl.BlockSpec(memory_space=pltpu.SMEM)] + [hbm] * 4,
        out_specs=[vmem] * planes,
        scratch_shapes=[
            pltpu.VMEM((CAP * owners, npno, naux), jnp.bfloat16),
            pltpu.VMEM(last.shape, jnp.bfloat16),
            pltpu.VMEM((pairs * npno, LANES), jnp.float32),
            pltpu.SemaphoreType.DMA((4,)),
        ],
        compiler_params=pltpu.CompilerParams(vmem_limit_bytes=60 * 2**20),
        name="exchange",
    )(place, first, above, last, below)


def body(
    ints_block,
    pair_vectors,
    pair_orbitals,
    orbital_place,
    amplitudes,
    pno_energy,
    occupied_fock_diagonal,
):
    n_orb = lax.axis_size("orb")
    n_rep = lax.axis_size("rep")
    rep = lax.axis_index("rep")
    keeper, naux, npao = ints_block.shape
    pair_dev = pair_vectors.shape[0]
    npno = pair_vectors.shape[2]
    vectors = pair_vectors.reshape(2 * pair_dev, npno, npao)

    def shifted(value, by):
        return lax.ppermute(value, "rep", [(i, (i + by) % n_rep) for i in range(n_rep)])

    def there(value):
        return lax.all_to_all(value, "orb", split_axis=0, concat_axis=0, tiled=True)

    sent, slot = route(
        pair_orbitals.T, orbital_place, rep.reshape(1).astype(jnp.int32), vectors, n_orb, keeper
    )
    own = there(sent)

    above, below = hold(shifted(ints_block, n_rep - 1), shifted(ints_block, 1))
    own, above, below = lax.optimization_barrier((own, above, below))
    opposite = shifted(own, 2)

    near, rest = near_halves(own, ints_block, above, below, npno)
    near = there(near)
    last, near = lax.optimization_barrier((far_halves(opposite, ints_block, rest, npno), near))
    last = there(last)

    main = npno // 16 * 16
    first = near[:, :main]
    above = shifted(near[:, main + npno :], n_rep - 1)
    below = shifted(near[:, main : main + npno], 1)
    place = (slot // n_orb - rep) % n_rep * n_orb + slot % n_orb
    mine = pair_dev // n_rep
    place = jnp.roll(place.reshape(n_rep, 2 * mine), -rep, axis=0).reshape(-1)
    products = exchange_of(place, n_rep, first, above, last, below)
    exchange = products[0]
    for by in (2, 1, n_rep - 1):
        exchange = exchange + shifted(products[by], by)
    own_orbs = lax.dynamic_slice_in_dim(pair_orbitals, rep * mine, mine, 0)
    first_fock = occupied_fock_diagonal[own_orbs[:, 0]]
    second_fock = occupied_fock_diagonal[own_orbs[:, 1]]
    gap = pno_energy[:, :, None] + pno_energy[:, None, :] - (first_fock + second_fock)[:, None, None]
    return exchange + gap.reshape(mine, npno * npno) * amplitudes.astype(jnp.float32)


def solution(mesh):
    placed = (
        P("orb", "rep", None),
        P("orb", None, None, None),
        P("orb", None),
        P(),
        P(("orb", "rep"), None),
        P(("orb", "rep"), None),
        P(),
    )
    return jax.shard_map(
        body, mesh=mesh, in_specs=placed, out_specs=P(("orb", "rep"), None), check_vma=False
    )
```

```python
import functools

import jax
import jax.numpy as jnp
from jax import lax
from jax.experimental import pallas as pl
from jax.experimental.pallas import tpu as pltpu
from jax.sharding import PartitionSpec as P

CAP = 4
TOGETHER = 8


LANES = 128
SPARE = 8
PARTS = 4


def pieces(npno, npao):
    whole = npno // 16 * 16
    blocks = npao // LANES
    cuts = []
    for c in range(blocks):
        lanes = slice(c * LANES, (c + 1) * LANES)
        cuts.append((slice(0, whole), lanes, slice(c * whole, (c + 1) * whole)))
        if npno > whole:
            at = blocks * whole + c * (npno - whole)
            cuts.append((slice(whole, npno), lanes, slice(at, at + npno - whole)))
    return cuts


def parted(at, keeper):
    if keeper & (keeper - 1):
        return lax.div(at, keeper), lax.rem(at, keeper)
    return lax.shift_right_logical(at, keeper.bit_length() - 1), lax.bitwise_and(at, keeper - 1)


def route_kernel(
    keeper, orbitals, place, plane, vectors, sent, slot, count, row, held, record, sems
):
    owners, npno, npao = held.shape
    pairs = orbitals.shape[1]
    together = 8

    def clear(o, _):
        count[o] = 0
        row[o] = keeper
        return 0

    lax.fori_loop(0, owners, clear, 0, unroll=16)
    mine = plane[0]

    def fetch(e, owner):
        return pltpu.make_async_copy(vectors.at[e], held.at[owner], sems.at[0])

    def some(g, _):
        for k in range(together):
            q = g * together + k
            for side in range(2):
                owner, of = parted(place[orbitals[side, q]], keeper)
                position = count[owner]
                count[owner] = position + 1
                slot[q * 2 + side] = position * owners + owner

                @pl.when(position == mine)
                def _():
                    row[owner] = of
                    fetch(q * 2 + side, owner).start()

        return 0

    lax.fori_loop(0, pairs // together, some, 0)

    def arrive(o, _):
        @pl.when(row[o] < keeper)
        def _():
            fetch(0, 0).wait()

        return 0

    lax.fori_loop(0, owners, arrive, 0, unroll=8)

    def lay(o, _):
        for rows, lanes, at in pieces(npno, npao):
            record[o, at, :] = held[o, rows, lanes]
        number = jnp.full((SPARE, LANES), row[o], jnp.int32).astype(jnp.float32)
        record[o, npno * npao // LANES :, :] = number.astype(record.dtype)
        return 0

    outs = []
    for part in range(PARTS):
        own = pl.ds(part * owners // PARTS, owners // PARTS)
        lax.fori_loop(part * owners // PARTS, (part + 1) * owners // PARTS, lay, 0, unroll=2)
        outs.append(pltpu.make_async_copy(record.at[own], sent.at[own], sems.at[1 + part]))
        outs[-1].start()
    for out in outs:
        out.wait()


def route(orbitals, orbital_place, plane, vectors, owners, keeper):
    entries, npno, npao = vectors.shape
    depth = npno * npao // LANES + SPARE
    smem = pl.BlockSpec(memory_space=pltpu.SMEM)
    hbm = pl.BlockSpec(memory_space=pltpu.HBM)
    return pl.pallas_call(
        functools.partial(route_kernel, keeper),
        out_shape=(
            jax.ShapeDtypeStruct((owners, depth, LANES), vectors.dtype),
            jax.ShapeDtypeStruct((entries,), jnp.int32),
        ),
        in_specs=[smem, smem, smem, hbm],
        out_specs=(hbm, smem),
        scratch_shapes=[
            pltpu.SMEM((owners,), jnp.int32),
            pltpu.SMEM((owners,), jnp.int32),
            pltpu.VMEM((owners, npno, npao), vectors.dtype),
            pltpu.VMEM((owners, depth, LANES), vectors.dtype),
            pltpu.SemaphoreType.DMA((1 + PARTS,)),
        ],
        compiler_params=pltpu.CompilerParams(vmem_limit_bytes=60 * 2**20),
        name="route",
    )(orbitals, orbital_place, plane, vectors)


def sort_entries(held, number, row, count, order, sem, keeper, at):
    items = held.shape[0]
    tile = held[:, at:, :].astype(jnp.float32)
    own = lax.broadcasted_iota(jnp.int32, tile.shape, 0)
    lane = lax.broadcasted_iota(jnp.int32, tile.shape, 2)
    number[...] = jnp.sum(jnp.where(own == lane, tile, 0.0), axis=0).astype(jnp.int32)
    move = pltpu.make_async_copy(number, row, sem)
    move.start()
    move.wait()
    for o in range(keeper + 1):
        count[o] = 0

    def sort(e, _):
        o = row[0, e]
        n = count[o]
        order[o * items + n] = e
        count[o] = n + 1
        return 0

    lax.fori_loop(0, items, sort, 0, unroll=8)


def stack(stacked, held, ids, npno):
    npao = stacked.shape[2]
    for t, e in enumerate(ids):
        for rows, lanes, at in pieces(npno, npao):
            stacked[t, rows, lanes] = held[e, at, :]
    return stacked[...].reshape(-1, npao)


def near_kernel(
    npno, held, own, above, below, out, rest_out,
    order, count, number, row, stacked, blocks, halves, rest, sems,
):
    keeper, naux, npao = own.shape
    items, tail, _ = rest.shape
    main = npno - tail
    loads = [
        pltpu.make_async_copy(
            share.at[o], blocks.at[o, pl.ds(k * naux, naux)], sems.at[4 + 3 * o + k]
        )
        for o in range(keeper)
        for k, share in enumerate((own, above, below))
    ]
    for load in loads:
        load.start()
    sort_entries(held, number, row, count, order, sems.at[1], keeper, npno * npao // LANES)

    def goes(e):
        return pltpu.make_async_copy(halves.at[e], out.at[e], sems.at[2])

    for o in range(keeper):
        for k in range(3):
            loads[3 * o + k].wait()
        n = count[o]

        def block(b, _):
            at = [b * TOGETHER + t for t in range(TOGETHER)]
            ids = [order[o * items + jnp.minimum(k, n - 1)] for k in at]
            for t, e in enumerate(ids):
                for rows, lanes, place in pieces(npno, npao):
                    stacked[t * npno + rows.start : t * npno + rows.stop, lanes] = held[e, place, :]
            value = lax.dot_general(
                stacked[...], blocks[o], (((1,), (1,)), ((), ())), preferred_element_type=jnp.float32
            )
            for t, e in enumerate(ids):
                rows = value[t * npno : (t + 1) * npno].astype(out.dtype)
                halves[e, :main] = rows[:main, :naux]
                rest[e] = rows[main:, :naux]
                halves[e, main : main + npno] = rows[:, naux : 2 * naux]
                halves[e, main + npno :] = rows[:, 2 * naux :]
            for k, e in zip(at, ids):

                @pl.when(k < n)
                def _():
                    goes(e).start()

            return 0

        lax.fori_loop(0, (n + TOGETHER - 1) // TOGETHER, block, 0)

    back = pltpu.make_async_copy(rest, rest_out, sems.at[3])
    back.start()

    def arrive(e, _):
        goes(0).wait()
        return 0

    lax.fori_loop(0, items - count[keeper], arrive, 0)
    back.wait()


def near_halves(record, own, above, below, npno):
    keeper, naux, npao = own.shape
    items = record.shape[0]
    tail = npno % 16
    rows = 3 * npno - tail
    hbm = pl.BlockSpec(memory_space=pltpu.HBM)
    return pl.pallas_call(
        functools.partial(near_kernel, npno),
        out_shape=[
            jax.ShapeDtypeStruct((items, rows, naux), jnp.bfloat16),
            jax.ShapeDtypeStruct((items, tail, naux), jnp.bfloat16),
        ],
        in_specs=[pl.BlockSpec(memory_space=pltpu.VMEM)] + [hbm] * 3,
        out_specs=[hbm] * 2,
        scratch_shapes=[
            pltpu.SMEM(((keeper + 1) * items,), jnp.int32),
            pltpu.SMEM((keeper + 1,), jnp.int32),
            pltpu.VMEM((SPARE, LANES), jnp.int32),
            pltpu.SMEM((SPARE, LANES), jnp.int32),
            pltpu.VMEM((TOGETHER * npno, npao), jnp.bfloat16),
            pltpu.VMEM((keeper, 3 * naux, npao), jnp.bfloat16),
            pltpu.VMEM((items, rows, naux), jnp.bfloat16),
            pltpu.VMEM((items, tail, naux), jnp.bfloat16),
            pltpu.SemaphoreType.DMA((4 + 3 * keeper,)),
        ],
        compiler_params=pltpu.CompilerParams(vmem_limit_bytes=48 * 2**20),
        cost_estimate=pl.CostEstimate(
            flops=6 * items * npno * npao * naux,
            bytes_accessed=2 * (3 * keeper * npao * naux + items * npno * (npao + 3 * naux)),
            transcendentals=0,
        ),
        name="near",
    )(record, own, above, below)


def far_kernel(npno, record, ints, rest_in, out, held, order, count, number, row, stacked, blocks, halves, rest, sems):
    keeper, naux, npao = ints.shape
    items = held.shape[0]
    deep = stacked.shape[1]
    whole = pltpu.make_async_copy(record, held, sems.at[0])
    load = pltpu.make_async_copy(ints, blocks, sems.at[1])
    rest_load = pltpu.make_async_copy(rest_in, rest, sems.at[2])
    for copy in (whole, load, rest_load):
        copy.start()
    stacked[...] = jnp.zeros_like(stacked)
    whole.wait()
    sort_entries(held, number, row, count, order, sems.at[3], keeper, npno * npao // LANES)
    load.wait()
    for o in range(keeper):
        n = count[o]

        def block(b, _):
            ids = [
                order[o * items + jnp.minimum(b * TOGETHER + t, n - 1)] for t in range(TOGETHER)
            ]
            value = lax.dot_general(
                stack(stacked, held, ids, npno),
                blocks[o],
                (((1,), (1,)), ((), ())),
                preferred_element_type=jnp.float32,
            ).astype(out.dtype)
            for t, e in enumerate(ids):
                halves[e, :npno] = value[t * deep : t * deep + npno]
            return 0

        lax.fori_loop(0, (n + TOGETHER - 1) // TOGETHER, block, 0)

    rest_load.wait()

    def join(e, _):
        halves[e, npno:] = rest[e]
        return 0

    lax.fori_loop(0, items, join, 0, unroll=8)
    back = pltpu.make_async_copy(halves, out, sems.at[4])
    back.start()
    back.wait()


def far_halves(record, ints, rest, npno):
    keeper, naux, npao = ints.shape
    items, tail, _ = rest.shape
    hbm = pl.BlockSpec(memory_space=pltpu.HBM)
    return pl.pallas_call(
        functools.partial(far_kernel, npno),
        out_shape=jax.ShapeDtypeStruct((items, npno + tail, naux), jnp.bfloat16),
        in_specs=[hbm] * 3,
        out_specs=hbm,
        scratch_shapes=[
            pltpu.VMEM(record.shape, record.dtype),
            pltpu.SMEM(((keeper + 1) * items,), jnp.int32),
            pltpu.SMEM((keeper + 1,), jnp.int32),
            pltpu.VMEM((SPARE, LANES), jnp.int32),
            pltpu.SMEM((SPARE, LANES), jnp.int32),
            pltpu.VMEM((TOGETHER, -(-npno // 16) * 16, npao), jnp.bfloat16),
            pltpu.VMEM(ints.shape, jnp.bfloat16),
            pltpu.VMEM((items, npno + tail, naux), jnp.bfloat16),
            pltpu.VMEM(rest.shape, jnp.bfloat16),
            pltpu.SemaphoreType.DMA((5,)),
        ],
        compiler_params=pltpu.CompilerParams(vmem_limit_bytes=60 * 2**20),
        cost_estimate=pl.CostEstimate(
            flops=16 * items * npno * npao * naux,
            bytes_accessed=2 * (keeper * npao * naux + items * npno * (npao + naux)),
            transcendentals=0,
        ),
        name="far",
    )(record, ints, rest)


def hold_kernel(above_in, below_in, above, below):
    pass


def hold(above, below):
    hbm = pl.BlockSpec(memory_space=pltpu.HBM)
    return pl.pallas_call(
        hold_kernel,
        out_shape=[jax.ShapeDtypeStruct(above.shape, above.dtype)] * 2,
        in_specs=[hbm] * 2,
        out_specs=[hbm] * 2,
        input_output_aliases={0: 0, 1: 1},
        compiler_params=pltpu.CompilerParams(vmem_limit_bytes=60 * 2**20),
        cost_estimate=pl.CostEstimate(flops=10**11, bytes_accessed=0, transcendentals=0),
        name="hold",
    )(above, below)


def exchange_kernel(place, first, above, last, below, *refs):
    planes = len(refs) - 4
    outs, (halves, late, product, sems) = refs[:planes], refs[planes:]
    owners, main, _ = first.shape
    npno = halves.shape[1]
    copies = [
        pltpu.make_async_copy(last, late, sems.at[0]),
        pltpu.make_async_copy(
            first, halves.at[pl.ds(0, owners), pl.ds(0, main)], sems.at[1]
        ),
        pltpu.make_async_copy(above, halves.at[pl.ds(owners, owners)], sems.at[2]),
        pltpu.make_async_copy(below, halves.at[pl.ds(3 * owners, owners)], sems.at[3]),
    ]
    for copy in copies:
        copy.start()
    copies[0].wait()

    def join(e, _):
        halves[e, main:] = late[e, npno:]
        halves[2 * owners + e] = late[e, :npno]
        return 0

    lax.fori_loop(0, owners, join, 0, unroll=4)
    for copy in copies[1:]:
        copy.wait()
    each = outs[0].shape[0]

    def some(g, _):
        for k in range(each):
            q = g * each + k
            at = pl.multiple_of(q * npno, 8)
            product[pl.ds(at, npno), :npno] = lax.dot_general(
                halves[place[2 * q]],
                halves[place[2 * q + 1]],
                (((1,), (1,)), ((), ())),
                preferred_element_type=jnp.float32,
            )
        return 0

    lax.fori_loop(0, planes, some, 0)
    for g in range(planes):
        for x in range(npno):
            rows = product[pl.ds(g * each * npno + x, each, stride=npno), :]
            outs[g][:, x * npno : (x + 1) * npno] = rows[:, :npno]


def exchange_of(place, planes, first, above, last, below):
    owners, npno, naux = above.shape
    pairs = place.shape[0] // 2
    hbm = pl.BlockSpec(memory_space=pltpu.HBM)
    vmem = pl.BlockSpec(memory_space=pltpu.VMEM)
    out = jax.ShapeDtypeStruct((pairs // planes, npno * npno), jnp.float32)
    return pl.pallas_call(
        exchange_kernel,
        out_shape=[out] * planes,
        in_specs=[pl.BlockSpec(memory_space=pltpu.SMEM)] + [hbm] * 4,
        out_specs=[vmem] * planes,
        scratch_shapes=[
            pltpu.VMEM((CAP * owners, npno, naux), jnp.bfloat16),
            pltpu.VMEM(last.shape, jnp.bfloat16),
            pltpu.VMEM((pairs * npno, LANES), jnp.float32),
            pltpu.SemaphoreType.DMA((4,)),
        ],
        compiler_params=pltpu.CompilerParams(vmem_limit_bytes=48 * 2**20),
        name="exchange",
    )(place, first, above, last, below)


def body(
    ints_block,
    pair_vectors,
    pair_orbitals,
    orbital_place,
    amplitudes,
    pno_energy,
    occupied_fock_diagonal,
):
    n_orb = lax.axis_size("orb")
    n_rep = lax.axis_size("rep")
    rep = lax.axis_index("rep")
    keeper, naux, npao = ints_block.shape
    pair_dev = pair_vectors.shape[0]
    npno = pair_vectors.shape[2]
    vectors = pair_vectors.reshape(2 * pair_dev, npno, npao)

    def shifted(value, by):
        return lax.ppermute(value, "rep", [(i, (i + by) % n_rep) for i in range(n_rep)])

    def there(value):
        return lax.all_to_all(value, "orb", split_axis=0, concat_axis=0, tiled=True)

    sent, slot = route(
        pair_orbitals.T, orbital_place, rep.reshape(1).astype(jnp.int32), vectors, n_orb, keeper
    )
    own = there(sent)

    above, below = hold(shifted(ints_block, n_rep - 1), shifted(ints_block, 1))
    own, above, below = lax.optimization_barrier((own, above, below))
    opposite = shifted(own, 2)

    near, rest = near_halves(own, ints_block, above, below, npno)
    near = there(near)
    last, near = lax.optimization_barrier((far_halves(opposite, ints_block, rest, npno), near))
    last = there(last)

    main = npno // 16 * 16
    first = near[:, :main]
    above = shifted(near[:, main + npno :], n_rep - 1)
    below = shifted(near[:, main : main + npno], 1)
    place = (slot // n_orb - rep) % n_rep * n_orb + slot % n_orb
    mine = pair_dev // n_rep
    own_orbs = lax.dynamic_slice_in_dim(pair_orbitals, rep * mine, mine, 0)
    first_fock = occupied_fock_diagonal[own_orbs[:, 0]]
    second_fock = occupied_fock_diagonal[own_orbs[:, 1]]
    gap = pno_energy[:, :, None] + pno_energy[:, None, :] - (first_fock + second_fock)[:, None, None]
    local = gap.reshape(mine, npno * npno) * amplitudes.astype(jnp.float32)
    last, local = lax.optimization_barrier((last, local))
    place = jnp.roll(place.reshape(n_rep, 2 * mine), -rep, axis=0).reshape(-1)
    products = exchange_of(place, n_rep, first, above, last, below)
    exchange = products[0]
    for by in (2, 1, n_rep - 1):
        exchange = exchange + shifted(products[by], by)
    return exchange + local


def solution(mesh):
    placed = (
        P("orb", "rep", None),
        P("orb", None, None, None),
        P("orb", None),
        P(),
        P(("orb", "rep"), None),
        P(("orb", "rep"), None),
        P(),
    )
    return jax.shard_map(
        body, mesh=mesh, in_specs=placed, out_specs=P(("orb", "rep"), None), check_vma=False
    )
```

```python
import functools

import jax
import jax.numpy as jnp
from jax import lax
from jax.experimental import pallas as pl
from jax.experimental.pallas import tpu as pltpu
from jax.sharding import PartitionSpec as P

CAP = 4
TOGETHER = 8
SIZES = (6, 12)


LANES = 128
SPARE = 8
PARTS = 4


def pieces(npno, npao):
    whole = npno // 16 * 16
    blocks = npao // LANES
    cuts = []
    for c in range(blocks):
        lanes = slice(c * LANES, (c + 1) * LANES)
        cuts.append((slice(0, whole), lanes, slice(c * whole, (c + 1) * whole)))
        if npno > whole:
            at = blocks * whole + c * (npno - whole)
            cuts.append((slice(whole, npno), lanes, slice(at, at + npno - whole)))
    return cuts


def parted(at, keeper):
    if keeper & (keeper - 1):
        return lax.div(at, keeper), lax.rem(at, keeper)
    return lax.shift_right_logical(at, keeper.bit_length() - 1), lax.bitwise_and(at, keeper - 1)


def route_kernel(
    keeper, orbitals, place, plane, vectors, sent, slot, count, row, held, record, sems
):
    owners, npno, npao = held.shape
    pairs = orbitals.shape[1]
    together = 8

    def clear(o, _):
        count[o] = 0
        row[o] = keeper
        return 0

    lax.fori_loop(0, owners, clear, 0, unroll=16)
    mine = plane[0]

    def fetch(e, owner):
        return pltpu.make_async_copy(vectors.at[e], held.at[owner], sems.at[0])

    def some(g, _):
        for k in range(together):
            q = g * together + k
            for side in range(2):
                owner, of = parted(place[orbitals[side, q]], keeper)
                position = count[owner]
                count[owner] = position + 1
                slot[q * 2 + side] = position * owners + owner

                @pl.when(position == mine)
                def _():
                    row[owner] = of
                    fetch(q * 2 + side, owner).start()

        return 0

    lax.fori_loop(0, pairs // together, some, 0)

    def arrive(o, _):
        @pl.when(row[o] < keeper)
        def _():
            fetch(0, 0).wait()

        return 0

    lax.fori_loop(0, owners, arrive, 0, unroll=8)

    def lay(o, _):
        for rows, lanes, at in pieces(npno, npao):
            record[o, at, :] = held[o, rows, lanes]
        number = jnp.full((SPARE, LANES), row[o], jnp.int32).astype(jnp.float32)
        record[o, npno * npao // LANES :, :] = number.astype(record.dtype)
        return 0

    outs = []
    for part in range(PARTS):
        own = pl.ds(part * owners // PARTS, owners // PARTS)
        lax.fori_loop(part * owners // PARTS, (part + 1) * owners // PARTS, lay, 0, unroll=2)
        outs.append(pltpu.make_async_copy(record.at[own], sent.at[own], sems.at[1 + part]))
        outs[-1].start()
    for out in outs:
        out.wait()


def route(orbitals, orbital_place, plane, vectors, owners, keeper):
    entries, npno, npao = vectors.shape
    depth = npno * npao // LANES + SPARE
    smem = pl.BlockSpec(memory_space=pltpu.SMEM)
    hbm = pl.BlockSpec(memory_space=pltpu.HBM)
    return pl.pallas_call(
        functools.partial(route_kernel, keeper),
        out_shape=(
            jax.ShapeDtypeStruct((owners, depth, LANES), vectors.dtype),
            jax.ShapeDtypeStruct((entries,), jnp.int32),
        ),
        in_specs=[smem, smem, smem, hbm],
        out_specs=(hbm, smem),
        scratch_shapes=[
            pltpu.SMEM((owners,), jnp.int32),
            pltpu.SMEM((owners,), jnp.int32),
            pltpu.VMEM((owners, npno, npao), vectors.dtype),
            pltpu.VMEM((owners, depth, LANES), vectors.dtype),
            pltpu.SemaphoreType.DMA((1 + PARTS,)),
        ],
        compiler_params=pltpu.CompilerParams(vmem_limit_bytes=60 * 2**20),
        name="route",
    )(orbitals, orbital_place, plane, vectors)


def sort_entries(held, number, row, count, order, sem, keeper, at):
    items = held.shape[0]
    tile = held[:, at:, :].astype(jnp.float32)
    own = lax.broadcasted_iota(jnp.int32, tile.shape, 0)
    lane = lax.broadcasted_iota(jnp.int32, tile.shape, 2)
    number[...] = jnp.sum(jnp.where(own == lane, tile, 0.0), axis=0).astype(jnp.int32)
    move = pltpu.make_async_copy(number, row, sem)
    move.start()
    move.wait()
    for o in range(keeper + 1):
        count[o] = 0

    def sort(e, _):
        o = row[0, e]
        n = count[o]
        order[o * items + n] = e
        count[o] = n + 1
        return 0

    lax.fori_loop(0, items, sort, 0, unroll=8)


def stack(stacked, held, ids, npno):
    npao = stacked.shape[2]
    for t, e in enumerate(ids):
        for rows, lanes, at in pieces(npno, npao):
            stacked[t, rows, lanes] = held[e, at, :]
    return stacked[...].reshape(-1, npao)


def near_kernel(
    npno, held, own, above, below, out, rest_out,
    order, count, number, row, stacked, blocks, halves, rest, sems,
):
    keeper, naux, npao = own.shape
    items, tail, _ = rest.shape
    main = npno - tail

    def loads(o):
        return [
            pltpu.make_async_copy(
                share.at[o], blocks.at[o, pl.ds(k * naux, naux)], sems.at[4 + 3 * o + k]
            )
            for k, share in enumerate((own, above, below))
        ]

    for o in range(keeper):
        for load in loads(o):
            load.start()
    sort_entries(held, number, row, count, order, sems.at[1], keeper, npno * npao // LANES)

    def goes(e):
        return pltpu.make_async_copy(halves.at[e], out.at[e], sems.at[2])

    def orbital(o, _):
        for load in loads(o):
            load.wait()
        n = count[o]

        def block(first, size):
            at = [first + t for t in range(size)]
            ids = [order[o * items + jnp.minimum(k, n - 1)] for k in at]
            for t, e in enumerate(ids):
                for rows, lanes, place in pieces(npno, npao):
                    stacked[t * npno + rows.start : t * npno + rows.stop, lanes] = held[e, place, :]
            value = lax.dot_general(
                stacked[: size * npno],
                blocks[o],
                (((1,), (1,)), ((), ())),
                preferred_element_type=jnp.float32,
            )
            for t, e in enumerate(ids):
                rows = value[t * npno : (t + 1) * npno].astype(out.dtype)
                halves[e, :main] = rows[:main, :naux]
                rest[e] = rows[main:, :naux]
                halves[e, main : main + npno] = rows[:, naux : 2 * naux]
                halves[e, main + npno :] = rows[:, 2 * naux :]
            for k, e in zip(at, ids):

                @pl.when(k < n)
                def _():
                    goes(e).start()

        most = SIZES[-1]
        if len(SIZES) == 1:

            def wide(b, _):
                block(b * most, most)
                return 0

            lax.fori_loop(0, (n + most - 1) // most, wide, 0)
        else:
            whole = (n + most - SIZES[0] - 1) // most

            def wide(b, _):
                block(b * most, most)
                return 0

            lax.fori_loop(0, whole, wide, 0)

            @pl.when(n > whole * most)
            def _():
                block(whole * most, SIZES[0])

        return 0

    lax.fori_loop(0, keeper, orbital, 0)

    back = pltpu.make_async_copy(rest, rest_out, sems.at[3])
    back.start()

    def arrive(e, _):
        goes(0).wait()
        return 0

    lax.fori_loop(0, items - count[keeper], arrive, 0)
    back.wait()


def near_halves(record, own, above, below, npno):
    keeper, naux, npao = own.shape
    items = record.shape[0]
    tail = npno % 16
    rows = 3 * npno - tail
    hbm = pl.BlockSpec(memory_space=pltpu.HBM)
    return pl.pallas_call(
        functools.partial(near_kernel, npno),
        out_shape=[
            jax.ShapeDtypeStruct((items, rows, naux), jnp.bfloat16),
            jax.ShapeDtypeStruct((items, tail, naux), jnp.bfloat16),
        ],
        in_specs=[pl.BlockSpec(memory_space=pltpu.VMEM)] + [hbm] * 3,
        out_specs=[hbm] * 2,
        scratch_shapes=[
            pltpu.SMEM(((keeper + 1) * items,), jnp.int32),
            pltpu.SMEM((keeper + 1,), jnp.int32),
            pltpu.VMEM((SPARE, LANES), jnp.int32),
            pltpu.SMEM((SPARE, LANES), jnp.int32),
            pltpu.VMEM((SIZES[-1] * npno, npao), jnp.bfloat16),
            pltpu.VMEM((keeper, 3 * naux, npao), jnp.bfloat16),
            pltpu.VMEM((items, rows, naux), jnp.bfloat16),
            pltpu.VMEM((items, tail, naux), jnp.bfloat16),
            pltpu.SemaphoreType.DMA((4 + 3 * keeper,)),
        ],
        compiler_params=pltpu.CompilerParams(vmem_limit_bytes=48 * 2**20),
        cost_estimate=pl.CostEstimate(
            flops=6 * items * npno * npao * naux,
            bytes_accessed=2 * (3 * keeper * npao * naux + items * npno * (npao + 3 * naux)),
            transcendentals=0,
        ),
        name="near",
    )(record, own, above, below)


def far_kernel(
    npno, held, ints, rest, out, order, count, number, row, stacked, blocks, halves, sems
):
    keeper, naux, npao = ints.shape
    items = held.shape[0]
    deep = stacked.shape[1]
    load = pltpu.make_async_copy(ints, blocks, sems.at[0])
    load.start()
    stacked[...] = jnp.zeros_like(stacked)
    sort_entries(held, number, row, count, order, sems.at[1], keeper, npno * npao // LANES)
    load.wait()
    for o in range(keeper):
        n = count[o]

        def block(b, _):
            ids = [
                order[o * items + jnp.minimum(b * TOGETHER + t, n - 1)] for t in range(TOGETHER)
            ]
            value = lax.dot_general(
                stack(stacked, held, ids, npno),
                blocks[o],
                (((1,), (1,)), ((), ())),
                preferred_element_type=jnp.float32,
            ).astype(out.dtype)
            for t, e in enumerate(ids):
                halves[e, :npno] = value[t * deep : t * deep + npno]
            return 0

        lax.fori_loop(0, (n + TOGETHER - 1) // TOGETHER, block, 0)

    def join(e, _):
        halves[e, npno:] = rest[e]
        return 0

    lax.fori_loop(0, items, join, 0, unroll=8)
    back = pltpu.make_async_copy(halves, out, sems.at[2])
    back.start()
    back.wait()


def far_halves(record, ints, rest, npno):
    keeper, naux, npao = ints.shape
    items, tail, _ = rest.shape
    hbm = pl.BlockSpec(memory_space=pltpu.HBM)
    vmem = pl.BlockSpec(memory_space=pltpu.VMEM)
    return pl.pallas_call(
        functools.partial(far_kernel, npno),
        out_shape=jax.ShapeDtypeStruct((items, npno + tail, naux), jnp.bfloat16),
        in_specs=[vmem, hbm, vmem],
        out_specs=hbm,
        scratch_shapes=[
            pltpu.SMEM(((keeper + 1) * items,), jnp.int32),
            pltpu.SMEM((keeper + 1,), jnp.int32),
            pltpu.VMEM((SPARE, LANES), jnp.int32),
            pltpu.SMEM((SPARE, LANES), jnp.int32),
            pltpu.VMEM((TOGETHER, -(-npno // 16) * 16, npao), jnp.bfloat16),
            pltpu.VMEM(ints.shape, jnp.bfloat16),
            pltpu.VMEM((items, npno + tail, naux), jnp.bfloat16),
            pltpu.SemaphoreType.DMA((3,)),
        ],
        compiler_params=pltpu.CompilerParams(vmem_limit_bytes=48 * 2**20),
        cost_estimate=pl.CostEstimate(
            flops=16 * items * npno * npao * naux,
            bytes_accessed=2 * (keeper * npao * naux + items * npno * (npao + naux)),
            transcendentals=0,
        ),
        name="far",
    )(record, ints, rest)


def hold_kernel(above_in, below_in, above, below):
    pass


def hold(above, below):
    hbm = pl.BlockSpec(memory_space=pltpu.HBM)
    return pl.pallas_call(
        hold_kernel,
        out_shape=[jax.ShapeDtypeStruct(above.shape, above.dtype)] * 2,
        in_specs=[hbm] * 2,
        out_specs=[hbm] * 2,
        input_output_aliases={0: 0, 1: 1},
        compiler_params=pltpu.CompilerParams(vmem_limit_bytes=60 * 2**20),
        cost_estimate=pl.CostEstimate(flops=10**11, bytes_accessed=0, transcendentals=0),
        name="hold",
    )(above, below)


def exchange_kernel(place, first, above, last, below, *refs):
    planes = len(refs) - 4
    outs, (halves, late, product, sems) = refs[:planes], refs[planes:]
    owners, main, _ = first.shape
    npno = halves.shape[1]
    copies = [
        pltpu.make_async_copy(last, late, sems.at[0]),
        pltpu.make_async_copy(
            first, halves.at[pl.ds(0, owners), pl.ds(0, main)], sems.at[1]
        ),
        pltpu.make_async_copy(above, halves.at[pl.ds(owners, owners)], sems.at[2]),
        pltpu.make_async_copy(below, halves.at[pl.ds(3 * owners, owners)], sems.at[3]),
    ]
    for copy in copies:
        copy.start()
    copies[0].wait()

    def join(e, _):
        halves[e, main:] = late[e, npno:]
        halves[2 * owners + e] = late[e, :npno]
        return 0

    lax.fori_loop(0, owners, join, 0, unroll=4)
    for copy in copies[1:]:
        copy.wait()
    each = outs[0].shape[0]

    def some(g, _):
        for k in range(each):
            q = g * each + k
            at = pl.multiple_of(q * npno, 8)
            product[pl.ds(at, npno), :npno] = lax.dot_general(
                halves[place[2 * q]],
                halves[place[2 * q + 1]],
                (((1,), (1,)), ((), ())),
                preferred_element_type=jnp.float32,
            )
        return 0

    lax.fori_loop(0, planes, some, 0)
    for g in range(planes):
        for x in range(npno):
            rows = product[pl.ds(g * each * npno + x, each, stride=npno), :]
            outs[g][:, x * npno : (x + 1) * npno] = rows[:, :npno]


def exchange_of(place, planes, first, above, last, below):
    owners, npno, naux = above.shape
    pairs = place.shape[0] // 2
    hbm = pl.BlockSpec(memory_space=pltpu.HBM)
    vmem = pl.BlockSpec(memory_space=pltpu.VMEM)
    out = jax.ShapeDtypeStruct((pairs // planes, npno * npno), jnp.float32)
    return pl.pallas_call(
        exchange_kernel,
        out_shape=[out] * planes,
        in_specs=[pl.BlockSpec(memory_space=pltpu.SMEM)] + [hbm] * 4,
        out_specs=[vmem] * planes,
        scratch_shapes=[
            pltpu.VMEM((CAP * owners, npno, naux), jnp.bfloat16),
            pltpu.VMEM(last.shape, jnp.bfloat16),
            pltpu.VMEM((pairs * npno, LANES), jnp.float32),
            pltpu.SemaphoreType.DMA((4,)),
        ],
        compiler_params=pltpu.CompilerParams(vmem_limit_bytes=48 * 2**20),
        name="exchange",
    )(place, first, above, last, below)


def body(
    ints_block,
    pair_vectors,
    pair_orbitals,
    orbital_place,
    amplitudes,
    pno_energy,
    occupied_fock_diagonal,
):
    n_orb = lax.axis_size("orb")
    n_rep = lax.axis_size("rep")
    rep = lax.axis_index("rep")
    keeper, naux, npao = ints_block.shape
    pair_dev = pair_vectors.shape[0]
    npno = pair_vectors.shape[2]
    vectors = pair_vectors.reshape(2 * pair_dev, npno, npao)

    def shifted(value, by):
        return lax.ppermute(value, "rep", [(i, (i + by) % n_rep) for i in range(n_rep)])

    def there(value):
        return lax.all_to_all(value, "orb", split_axis=0, concat_axis=0, tiled=True)

    sent, slot = route(
        pair_orbitals.T, orbital_place, rep.reshape(1).astype(jnp.int32), vectors, n_orb, keeper
    )
    own = there(sent)

    above, below = hold(shifted(ints_block, n_rep - 1), shifted(ints_block, 1))
    own, above, below = lax.optimization_barrier((own, above, below))
    opposite = shifted(own, 2)

    near, rest = near_halves(own, ints_block, above, below, npno)
    near = there(near)
    last, near = lax.optimization_barrier((far_halves(opposite, ints_block, rest, npno), near))
    last = there(last)

    main = npno // 16 * 16
    first = near[:, :main]
    above = shifted(near[:, main + npno :], n_rep - 1)
    below = shifted(near[:, main : main + npno], 1)
    place = (slot // n_orb - rep) % n_rep * n_orb + slot % n_orb
    mine = pair_dev // n_rep
    own_orbs = lax.dynamic_slice_in_dim(pair_orbitals, rep * mine, mine, 0)
    first_fock = occupied_fock_diagonal[own_orbs[:, 0]]
    second_fock = occupied_fock_diagonal[own_orbs[:, 1]]
    gap = pno_energy[:, :, None] + pno_energy[:, None, :] - (first_fock + second_fock)[:, None, None]
    local = gap.reshape(mine, npno * npno) * amplitudes.astype(jnp.float32)
    last, local = lax.optimization_barrier((last, local))
    place = jnp.roll(place.reshape(n_rep, 2 * mine), -rep, axis=0).reshape(-1)
    products = exchange_of(place, n_rep, first, above, last, below)
    exchange = products[0]
    for by in (2, 1, n_rep - 1):
        exchange = exchange + shifted(products[by], by)
    return exchange + local


def solution(mesh):
    placed = (
        P("orb", "rep", None),
        P("orb", None, None, None),
        P("orb", None),
        P(),
        P(("orb", "rep"), None),
        P(("orb", "rep"), None),
        P(),
    )
    return jax.shard_map(
        body, mesh=mesh, in_specs=placed, out_specs=P(("orb", "rep"), None), check_vma=False
    )
```

```python
import functools

import jax
import jax.numpy as jnp
from jax import lax
from jax.experimental import pallas as pl
from jax.experimental.pallas import tpu as pltpu
from jax.sharding import PartitionSpec as P

CAP = 4
TOGETHER = 8
SIZES = (8, 12)


LANES = 128
SPARE = 8
PARTS = 4


def pieces(npno, npao):
    whole = npno // 16 * 16
    blocks = npao // LANES
    cuts = []
    for c in range(blocks):
        lanes = slice(c * LANES, (c + 1) * LANES)
        cuts.append((slice(0, whole), lanes, slice(c * whole, (c + 1) * whole)))
        if npno > whole:
            at = blocks * whole + c * (npno - whole)
            cuts.append((slice(whole, npno), lanes, slice(at, at + npno - whole)))
    return cuts


def parted(at, keeper):
    if keeper & (keeper - 1):
        return lax.div(at, keeper), lax.rem(at, keeper)
    return lax.shift_right_logical(at, keeper.bit_length() - 1), lax.bitwise_and(at, keeper - 1)


def route_kernel(
    keeper, orbitals, place, plane, source, vectors, sent, slot, count, row, held, record, sems
):
    owners, npno, npao = held.shape
    pairs = orbitals.shape[1]
    together = 8

    def clear(o, _):
        count[o] = 0
        row[o] = keeper
        return 0

    lax.fori_loop(0, owners, clear, 0, unroll=16)
    mine, turn = plane[0], source[0]

    def fetch(e, owner):
        return pltpu.make_async_copy(vectors.at[e], held.at[owner], sems.at[0])

    def some(g, _):
        for k in range(together):
            q = g * together + k
            for side in range(2):
                owner, of = parted(place[orbitals[side, q]], keeper)
                position = count[owner]
                count[owner] = position + 1
                turned = parted(position + owner + turn, CAP)[1]
                slot[q * 2 + side] = turned * owners + owner

                @pl.when(turned == mine)
                def _():
                    row[owner] = of
                    fetch(q * 2 + side, owner).start()

        return 0

    lax.fori_loop(0, pairs // together, some, 0)

    def arrive(o, _):
        @pl.when(row[o] < keeper)
        def _():
            fetch(0, 0).wait()

        return 0

    lax.fori_loop(0, owners, arrive, 0, unroll=8)

    def lay(o, _):
        for rows, lanes, at in pieces(npno, npao):
            record[o, at, :] = held[o, rows, lanes]
        number = jnp.full((SPARE, LANES), row[o], jnp.int32).astype(jnp.float32)
        record[o, npno * npao // LANES :, :] = number.astype(record.dtype)
        return 0

    outs = []
    for part in range(PARTS):
        own = pl.ds(part * owners // PARTS, owners // PARTS)
        lax.fori_loop(part * owners // PARTS, (part + 1) * owners // PARTS, lay, 0, unroll=2)
        outs.append(pltpu.make_async_copy(record.at[own], sent.at[own], sems.at[1 + part]))
        outs[-1].start()
    for out in outs:
        out.wait()


def route(orbitals, orbital_place, at, vectors, owners, keeper):
    entries, npno, npao = vectors.shape
    depth = npno * npao // LANES + SPARE
    smem = pl.BlockSpec(memory_space=pltpu.SMEM)
    hbm = pl.BlockSpec(memory_space=pltpu.HBM)
    return pl.pallas_call(
        functools.partial(route_kernel, keeper),
        out_shape=(
            jax.ShapeDtypeStruct((owners, depth, LANES), vectors.dtype),
            jax.ShapeDtypeStruct((entries,), jnp.int32),
        ),
        in_specs=[smem] * 4 + [hbm],
        out_specs=(hbm, smem),
        scratch_shapes=[
            pltpu.SMEM((owners,), jnp.int32),
            pltpu.SMEM((owners,), jnp.int32),
            pltpu.VMEM((owners, npno, npao), vectors.dtype),
            pltpu.VMEM((owners, depth, LANES), vectors.dtype),
            pltpu.SemaphoreType.DMA((1 + PARTS,)),
        ],
        compiler_params=pltpu.CompilerParams(vmem_limit_bytes=60 * 2**20),
        name="route",
    )(orbitals, orbital_place, *at, vectors)


def sort_entries(held, number, row, count, order, sem, keeper, at):
    items = held.shape[0]
    tile = held[:, at:, :].astype(jnp.float32)
    own = lax.broadcasted_iota(jnp.int32, tile.shape, 0)
    lane = lax.broadcasted_iota(jnp.int32, tile.shape, 2)
    number[...] = jnp.sum(jnp.where(own == lane, tile, 0.0), axis=0).astype(jnp.int32)
    move = pltpu.make_async_copy(number, row, sem)
    move.start()
    move.wait()
    for o in range(keeper + 1):
        count[o] = 0

    def sort(e, _):
        o = row[0, e]
        n = count[o]
        order[o * items + n] = e
        count[o] = n + 1
        return 0

    lax.fori_loop(0, items, sort, 0, unroll=8)


def stack(stacked, held, ids, npno):
    npao = stacked.shape[2]
    for t, e in enumerate(ids):
        for rows, lanes, at in pieces(npno, npao):
            stacked[t, rows, lanes] = held[e, at, :]
    return stacked[...].reshape(-1, npao)


def near_kernel(
    npno, held, own, above, below, out, rest_out,
    order, count, number, row, stacked, blocks, halves, rest, sems,
):
    keeper, naux, npao = own.shape
    items, tail, _ = rest.shape
    main = npno - tail

    def loads(o):
        return [
            pltpu.make_async_copy(
                share.at[o], blocks.at[o, pl.ds(k * naux, naux)], sems.at[4 + 3 * o + k]
            )
            for k, share in enumerate((own, above, below))
        ]

    for o in range(keeper):
        for load in loads(o):
            load.start()
    sort_entries(held, number, row, count, order, sems.at[1], keeper, npno * npao // LANES)

    def goes(e):
        return pltpu.make_async_copy(halves.at[e], out.at[e], sems.at[2])

    def orbital(o, _):
        for load in loads(o):
            load.wait()
        n = count[o]

        def block(first, size):
            at = [first + t for t in range(size)]
            ids = [order[o * items + jnp.minimum(k, n - 1)] for k in at]
            for t, e in enumerate(ids):
                for rows, lanes, place in pieces(npno, npao):
                    stacked[t * npno + rows.start : t * npno + rows.stop, lanes] = held[e, place, :]
            value = lax.dot_general(
                stacked[: size * npno],
                blocks[o],
                (((1,), (1,)), ((), ())),
                preferred_element_type=jnp.float32,
            )
            for t, e in enumerate(ids):
                rows = value[t * npno : (t + 1) * npno].astype(out.dtype)
                halves[e, :main] = rows[:main, :naux]
                rest[e] = rows[main:, :naux]
                halves[e, main : main + npno] = rows[:, naux : 2 * naux]
                halves[e, main + npno :] = rows[:, 2 * naux :]
            for k, e in zip(at, ids):

                @pl.when(k < n)
                def _():
                    goes(e).start()

        most = SIZES[-1]
        if len(SIZES) == 1:

            def wide(b, _):
                block(b * most, most)
                return 0

            lax.fori_loop(0, (n + most - 1) // most, wide, 0)
        else:
            whole = (n + most - SIZES[0] - 1) // most

            def wide(b, _):
                block(b * most, most)
                return 0

            lax.fori_loop(0, whole, wide, 0)

            @pl.when(n > whole * most)
            def _():
                block(whole * most, SIZES[0])

        return 0

    lax.fori_loop(0, keeper, orbital, 0)

    back = pltpu.make_async_copy(rest, rest_out, sems.at[3])
    back.start()

    def arrive(e, _):
        goes(0).wait()
        return 0

    lax.fori_loop(0, items - count[keeper], arrive, 0)
    back.wait()


def near_halves(record, own, above, below, npno):
    keeper, naux, npao = own.shape
    items = record.shape[0]
    tail = npno % 16
    rows = 3 * npno - tail
    hbm = pl.BlockSpec(memory_space=pltpu.HBM)
    return pl.pallas_call(
        functools.partial(near_kernel, npno),
        out_shape=[
            jax.ShapeDtypeStruct((items, rows, naux), jnp.bfloat16),
            jax.ShapeDtypeStruct((items, tail, naux), jnp.bfloat16),
        ],
        in_specs=[pl.BlockSpec(memory_space=pltpu.VMEM)] + [hbm] * 3,
        out_specs=[hbm] * 2,
        scratch_shapes=[
            pltpu.SMEM(((keeper + 1) * items,), jnp.int32),
            pltpu.SMEM((keeper + 1,), jnp.int32),
            pltpu.VMEM((SPARE, LANES), jnp.int32),
            pltpu.SMEM((SPARE, LANES), jnp.int32),
            pltpu.VMEM((SIZES[-1] * npno, npao), jnp.bfloat16),
            pltpu.VMEM((keeper, 3 * naux, npao), jnp.bfloat16),
            pltpu.VMEM((items, rows, naux), jnp.bfloat16),
            pltpu.VMEM((items, tail, naux), jnp.bfloat16),
            pltpu.SemaphoreType.DMA((4 + 3 * keeper,)),
        ],
        compiler_params=pltpu.CompilerParams(vmem_limit_bytes=48 * 2**20),
        cost_estimate=pl.CostEstimate(
            flops=6 * items * npno * npao * naux,
            bytes_accessed=2 * (3 * keeper * npao * naux + items * npno * (npao + 3 * naux)),
            transcendentals=0,
        ),
        name="near",
    )(record, own, above, below)


def far_kernel(
    npno, held, ints, rest, out, order, count, number, row, stacked, blocks, halves, sems
):
    keeper, naux, npao = ints.shape
    items = held.shape[0]
    deep = stacked.shape[1]
    load = pltpu.make_async_copy(ints, blocks, sems.at[0])
    load.start()
    stacked[...] = jnp.zeros_like(stacked)
    sort_entries(held, number, row, count, order, sems.at[1], keeper, npno * npao // LANES)
    load.wait()
    for o in range(keeper):
        n = count[o]

        def block(b, _):
            ids = [
                order[o * items + jnp.minimum(b * TOGETHER + t, n - 1)] for t in range(TOGETHER)
            ]
            value = lax.dot_general(
                stack(stacked, held, ids, npno),
                blocks[o],
                (((1,), (1,)), ((), ())),
                preferred_element_type=jnp.float32,
            ).astype(out.dtype)
            for t, e in enumerate(ids):
                halves[e, :npno] = value[t * deep : t * deep + npno]
            return 0

        lax.fori_loop(0, (n + TOGETHER - 1) // TOGETHER, block, 0)

    def join(e, _):
        halves[e, npno:] = rest[e]
        return 0

    lax.fori_loop(0, items, join, 0, unroll=8)
    back = pltpu.make_async_copy(halves, out, sems.at[2])
    back.start()
    back.wait()


def far_halves(record, ints, rest, npno):
    keeper, naux, npao = ints.shape
    items, tail, _ = rest.shape
    hbm = pl.BlockSpec(memory_space=pltpu.HBM)
    vmem = pl.BlockSpec(memory_space=pltpu.VMEM)
    return pl.pallas_call(
        functools.partial(far_kernel, npno),
        out_shape=jax.ShapeDtypeStruct((items, npno + tail, naux), jnp.bfloat16),
        in_specs=[vmem, hbm, vmem],
        out_specs=hbm,
        scratch_shapes=[
            pltpu.SMEM(((keeper + 1) * items,), jnp.int32),
            pltpu.SMEM((keeper + 1,), jnp.int32),
            pltpu.VMEM((SPARE, LANES), jnp.int32),
            pltpu.SMEM((SPARE, LANES), jnp.int32),
            pltpu.VMEM((TOGETHER, -(-npno // 16) * 16, npao), jnp.bfloat16),
            pltpu.VMEM(ints.shape, jnp.bfloat16),
            pltpu.VMEM((items, npno + tail, naux), jnp.bfloat16),
            pltpu.SemaphoreType.DMA((3,)),
        ],
        compiler_params=pltpu.CompilerParams(vmem_limit_bytes=48 * 2**20),
        cost_estimate=pl.CostEstimate(
            flops=16 * items * npno * npao * naux,
            bytes_accessed=2 * (keeper * npao * naux + items * npno * (npao + naux)),
            transcendentals=0,
        ),
        name="far",
    )(record, ints, rest)


def hold_kernel(above_in, below_in, above, below):
    pass


def hold(above, below):
    hbm = pl.BlockSpec(memory_space=pltpu.HBM)
    return pl.pallas_call(
        hold_kernel,
        out_shape=[jax.ShapeDtypeStruct(above.shape, above.dtype)] * 2,
        in_specs=[hbm] * 2,
        out_specs=[hbm] * 2,
        input_output_aliases={0: 0, 1: 1},
        compiler_params=pltpu.CompilerParams(vmem_limit_bytes=60 * 2**20),
        cost_estimate=pl.CostEstimate(flops=10**11, bytes_accessed=0, transcendentals=0),
        name="hold",
    )(above, below)


def exchange_kernel(place, first, above, last, below, *refs):
    planes = len(refs) - 4
    outs, (halves, late, product, sems) = refs[:planes], refs[planes:]
    owners, main, _ = first.shape
    npno = halves.shape[1]
    copies = [
        pltpu.make_async_copy(last, late, sems.at[0]),
        pltpu.make_async_copy(
            first, halves.at[pl.ds(0, owners), pl.ds(0, main)], sems.at[1]
        ),
        pltpu.make_async_copy(above, halves.at[pl.ds(owners, owners)], sems.at[2]),
        pltpu.make_async_copy(below, halves.at[pl.ds(3 * owners, owners)], sems.at[3]),
    ]
    for copy in copies:
        copy.start()
    copies[0].wait()

    def join(e, _):
        halves[e, main:] = late[e, npno:]
        halves[2 * owners + e] = late[e, :npno]
        return 0

    lax.fori_loop(0, owners, join, 0, unroll=4)
    for copy in copies[1:]:
        copy.wait()
    each = outs[0].shape[0]

    def some(g, _):
        for k in range(each):
            q = g * each + k
            at = pl.multiple_of(q * npno, 8)
            product[pl.ds(at, npno), :npno] = lax.dot_general(
                halves[place[2 * q]],
                halves[place[2 * q + 1]],
                (((1,), (1,)), ((), ())),
                preferred_element_type=jnp.float32,
            )
        return 0

    lax.fori_loop(0, planes, some, 0)
    for g in range(planes):
        for x in range(npno):
            rows = product[pl.ds(g * each * npno + x, each, stride=npno), :]
            outs[g][:, x * npno : (x + 1) * npno] = rows[:, :npno]


def exchange_of(place, planes, first, above, last, below):
    owners, npno, naux = above.shape
    pairs = place.shape[0] // 2
    hbm = pl.BlockSpec(memory_space=pltpu.HBM)
    vmem = pl.BlockSpec(memory_space=pltpu.VMEM)
    out = jax.ShapeDtypeStruct((pairs // planes, npno * npno), jnp.float32)
    return pl.pallas_call(
        exchange_kernel,
        out_shape=[out] * planes,
        in_specs=[pl.BlockSpec(memory_space=pltpu.SMEM)] + [hbm] * 4,
        out_specs=[vmem] * planes,
        scratch_shapes=[
            pltpu.VMEM((CAP * owners, npno, naux), jnp.bfloat16),
            pltpu.VMEM(last.shape, jnp.bfloat16),
            pltpu.VMEM((pairs * npno, LANES), jnp.float32),
            pltpu.SemaphoreType.DMA((4,)),
        ],
        compiler_params=pltpu.CompilerParams(vmem_limit_bytes=48 * 2**20),
        name="exchange",
    )(place, first, above, last, below)


def body(
    ints_block,
    pair_vectors,
    pair_orbitals,
    orbital_place,
    amplitudes,
    pno_energy,
    occupied_fock_diagonal,
):
    n_orb = lax.axis_size("orb")
    n_rep = lax.axis_size("rep")
    rep = lax.axis_index("rep")
    at = [lax.axis_index(name).reshape(1).astype(jnp.int32) for name in ("rep", "orb")]
    keeper, naux, npao = ints_block.shape
    pair_dev = pair_vectors.shape[0]
    npno = pair_vectors.shape[2]
    vectors = pair_vectors.reshape(2 * pair_dev, npno, npao)

    def shifted(value, by):
        return lax.ppermute(value, "rep", [(i, (i + by) % n_rep) for i in range(n_rep)])

    def there(value):
        return lax.all_to_all(value, "orb", split_axis=0, concat_axis=0, tiled=True)

    sent, slot = route(
        pair_orbitals.T, orbital_place, at, vectors, n_orb, keeper
    )
    own = there(sent)

    above, below = hold(shifted(ints_block, n_rep - 1), shifted(ints_block, 1))
    own, above, below = lax.optimization_barrier((own, above, below))
    opposite = shifted(own, 2)

    near, rest = near_halves(own, ints_block, above, below, npno)
    near = there(near)
    last, near = lax.optimization_barrier((far_halves(opposite, ints_block, rest, npno), near))
    last = there(last)

    main = npno // 16 * 16
    first = near[:, :main]
    above = shifted(near[:, main + npno :], n_rep - 1)
    below = shifted(near[:, main : main + npno], 1)
    place = (slot // n_orb - rep) % n_rep * n_orb + slot % n_orb
    mine = pair_dev // n_rep
    own_orbs = lax.dynamic_slice_in_dim(pair_orbitals, rep * mine, mine, 0)
    first_fock = occupied_fock_diagonal[own_orbs[:, 0]]
    second_fock = occupied_fock_diagonal[own_orbs[:, 1]]
    gap = pno_energy[:, :, None] + pno_energy[:, None, :] - (first_fock + second_fock)[:, None, None]
    local = gap.reshape(mine, npno * npno) * amplitudes.astype(jnp.float32)
    last, local = lax.optimization_barrier((last, local))
    place = jnp.roll(place.reshape(n_rep, 2 * mine), -rep, axis=0).reshape(-1)
    products = exchange_of(place, n_rep, first, above, last, below)
    exchange = products[0]
    for by in (2, 1, n_rep - 1):
        exchange = exchange + shifted(products[by], by)
    return exchange + local


def solution(mesh):
    placed = (
        P("orb", "rep", None),
        P("orb", None, None, None),
        P("orb", None),
        P(),
        P(("orb", "rep"), None),
        P(("orb", "rep"), None),
        P(),
    )
    return jax.shard_map(
        body, mesh=mesh, in_specs=placed, out_specs=P(("orb", "rep"), None), check_vma=False
    )
```

```python
import functools

import jax
import jax.numpy as jnp
from jax import lax
from jax.experimental import pallas as pl
from jax.experimental.pallas import tpu as pltpu
from jax.sharding import PartitionSpec as P

CAP = 4
TOGETHER = 8
SIZES = (8, 12)


LANES = 128
SPARE = 8
PARTS = 4


def pieces(npno, npao):
    whole = npno // 16 * 16
    blocks = npao // LANES
    cuts = []
    for c in range(blocks):
        lanes = slice(c * LANES, (c + 1) * LANES)
        cuts.append((slice(0, whole), lanes, slice(c * whole, (c + 1) * whole)))
        if npno > whole:
            at = blocks * whole + c * (npno - whole)
            cuts.append((slice(whole, npno), lanes, slice(at, at + npno - whole)))
    return cuts


def parted(at, keeper):
    if keeper & (keeper - 1):
        return lax.div(at, keeper), lax.rem(at, keeper)
    return lax.shift_right_logical(at, keeper.bit_length() - 1), lax.bitwise_and(at, keeper - 1)


def route_kernel(
    keeper, orbitals, place, plane, source, vectors, sent, slot, count, row, held, record, sems
):
    owners, npno, npao = held.shape
    pairs = orbitals.shape[1]
    together = 8

    def clear(o, _):
        count[o] = 0
        row[o] = keeper
        return 0

    lax.fori_loop(0, owners, clear, 0, unroll=16)
    mine, turn = plane[0], source[0]

    def fetch(e, owner):
        return pltpu.make_async_copy(vectors.at[e], held.at[owner], sems.at[0])

    def some(g, _):
        for k in range(together):
            q = g * together + k
            for side in range(2):
                owner, of = parted(place[orbitals[side, q]], keeper)
                position = count[owner]
                count[owner] = position + 1
                turned = parted(position + owner + turn, CAP)[1]
                slot[q * 2 + side] = turned * owners + owner

                @pl.when(turned == mine)
                def _():
                    row[owner] = of
                    fetch(q * 2 + side, owner).start()

        return 0

    lax.fori_loop(0, pairs // together, some, 0)

    def arrive(o, _):
        @pl.when(row[o] < keeper)
        def _():
            fetch(0, 0).wait()

        return 0

    lax.fori_loop(0, owners, arrive, 0, unroll=8)

    def lay(o, _):
        for rows, lanes, at in pieces(npno, npao):
            record[o, at, :] = held[o, rows, lanes]
        number = jnp.full((SPARE, LANES), row[o], jnp.int32).astype(jnp.float32)
        record[o, npno * npao // LANES :, :] = number.astype(record.dtype)
        return 0

    outs = []
    for part in range(PARTS):
        own = pl.ds(part * owners // PARTS, owners // PARTS)
        lax.fori_loop(part * owners // PARTS, (part + 1) * owners // PARTS, lay, 0, unroll=2)
        outs.append(pltpu.make_async_copy(record.at[own], sent.at[own], sems.at[1 + part]))
        outs[-1].start()
    for out in outs:
        out.wait()


def route(orbitals, orbital_place, at, vectors, owners, keeper):
    entries, npno, npao = vectors.shape
    depth = npno * npao // LANES + SPARE
    smem = pl.BlockSpec(memory_space=pltpu.SMEM)
    hbm = pl.BlockSpec(memory_space=pltpu.HBM)
    return pl.pallas_call(
        functools.partial(route_kernel, keeper),
        out_shape=(
            jax.ShapeDtypeStruct((owners, depth, LANES), vectors.dtype),
            jax.ShapeDtypeStruct((entries,), jnp.int32),
        ),
        in_specs=[smem] * 4 + [hbm],
        out_specs=(hbm, smem),
        scratch_shapes=[
            pltpu.SMEM((owners,), jnp.int32),
            pltpu.SMEM((owners,), jnp.int32),
            pltpu.VMEM((owners, npno, npao), vectors.dtype),
            pltpu.VMEM((owners, depth, LANES), vectors.dtype),
            pltpu.SemaphoreType.DMA((1 + PARTS,)),
        ],
        compiler_params=pltpu.CompilerParams(vmem_limit_bytes=60 * 2**20),
        name="route",
    )(orbitals, orbital_place, *at, vectors)


def sort_entries(held, number, row, count, order, sem, keeper, at):
    items = held.shape[0]
    tile = held[:, at:, :].astype(jnp.float32)
    own = lax.broadcasted_iota(jnp.int32, tile.shape, 0)
    lane = lax.broadcasted_iota(jnp.int32, tile.shape, 2)
    number[...] = jnp.sum(jnp.where(own == lane, tile, 0.0), axis=0).astype(jnp.int32)
    move = pltpu.make_async_copy(number, row, sem)
    move.start()
    move.wait()
    for o in range(keeper + 1):
        count[o] = 0

    def sort(e, _):
        o = row[0, e]
        n = count[o]
        order[o * items + n] = e
        count[o] = n + 1
        return 0

    lax.fori_loop(0, items, sort, 0, unroll=8)


def stack(stacked, held, ids, npno):
    npao = stacked.shape[2]
    for t, e in enumerate(ids):
        for rows, lanes, at in pieces(npno, npao):
            stacked[t, rows, lanes] = held[e, at, :]
    return stacked[...].reshape(-1, npao)


def near_kernel(
    npno, held, own, above, below, out, rest_out,
    order, count, number, row, stacked, blocks, halves, rest, sems,
):
    keeper, naux, npao = own.shape
    items, tail, _ = rest.shape
    main = npno - tail

    def loads(o):
        return [
            pltpu.make_async_copy(
                share.at[o], blocks.at[o, pl.ds(k * naux, naux)], sems.at[4 + 3 * o + k]
            )
            for k, share in enumerate((own, above, below))
        ]

    for o in range(keeper):
        for load in loads(o):
            load.start()
    sort_entries(held, number, row, count, order, sems.at[1], keeper, npno * npao // LANES)

    def goes(e):
        return pltpu.make_async_copy(halves.at[e], out.at[e], sems.at[2])

    def orbital(o, _):
        for load in loads(o):
            load.wait()
        n = count[o]

        def block(first, size):
            at = [first + t for t in range(size)]
            ids = [order[o * items + jnp.minimum(k, n - 1)] for k in at]
            for t, e in enumerate(ids):
                for rows, lanes, place in pieces(npno, npao):
                    stacked[t * npno + rows.start : t * npno + rows.stop, lanes] = held[e, place, :]
            value = lax.dot_general(
                stacked[: size * npno],
                blocks[o],
                (((1,), (1,)), ((), ())),
                preferred_element_type=jnp.float32,
            )
            for t, e in enumerate(ids):
                rows = value[t * npno : (t + 1) * npno].astype(out.dtype)
                halves[e, :main] = rows[:main, :naux]
                rest[e] = rows[main:, :naux]
                halves[e, main : main + npno] = rows[:, naux : 2 * naux]
                halves[e, main + npno :] = rows[:, 2 * naux :]
            for k, e in zip(at, ids):

                @pl.when(k < n)
                def _():
                    goes(e).start()

        most = SIZES[-1]
        if len(SIZES) == 1:

            def wide(b, _):
                block(b * most, most)
                return 0

            lax.fori_loop(0, (n + most - 1) // most, wide, 0)
        else:
            whole = (n + most - SIZES[0] - 1) // most

            def wide(b, _):
                block(b * most, most)
                return 0

            lax.fori_loop(0, whole, wide, 0)

            @pl.when(n > whole * most)
            def _():
                block(whole * most, SIZES[0])

        return 0

    lax.fori_loop(0, keeper, orbital, 0)

    back = pltpu.make_async_copy(rest, rest_out, sems.at[3])
    back.start()

    def arrive(e, _):
        goes(0).wait()
        return 0

    lax.fori_loop(0, items - count[keeper], arrive, 0)
    back.wait()


def near_halves(record, own, above, below, npno):
    keeper, naux, npao = own.shape
    items = record.shape[0]
    tail = npno % 16
    rows = 3 * npno - tail
    hbm = pl.BlockSpec(memory_space=pltpu.HBM)
    return pl.pallas_call(
        functools.partial(near_kernel, npno),
        out_shape=[
            jax.ShapeDtypeStruct((items, rows, naux), jnp.bfloat16),
            jax.ShapeDtypeStruct((items, tail, naux), jnp.bfloat16),
        ],
        in_specs=[pl.BlockSpec(memory_space=pltpu.VMEM)] + [hbm] * 3,
        out_specs=[hbm] * 2,
        scratch_shapes=[
            pltpu.SMEM(((keeper + 1) * items,), jnp.int32),
            pltpu.SMEM((keeper + 1,), jnp.int32),
            pltpu.VMEM((SPARE, LANES), jnp.int32),
            pltpu.SMEM((SPARE, LANES), jnp.int32),
            pltpu.VMEM((SIZES[-1] * npno, npao), jnp.bfloat16),
            pltpu.VMEM((keeper, 3 * naux, npao), jnp.bfloat16),
            pltpu.VMEM((items, rows, naux), jnp.bfloat16),
            pltpu.VMEM((items, tail, naux), jnp.bfloat16),
            pltpu.SemaphoreType.DMA((4 + 3 * keeper,)),
        ],
        compiler_params=pltpu.CompilerParams(vmem_limit_bytes=48 * 2**20),
        cost_estimate=pl.CostEstimate(
            flops=6 * items * npno * npao * naux,
            bytes_accessed=2 * (3 * keeper * npao * naux + items * npno * (npao + 3 * naux)),
            transcendentals=0,
        ),
        name="near",
    )(record, own, above, below)


def far_kernel(
    npno, held, ints, rest, out, order, count, number, row, stacked, blocks, halves, sems
):
    keeper, naux, npao = ints.shape
    items = held.shape[0]
    deep = stacked.shape[1]
    load = pltpu.make_async_copy(ints, blocks, sems.at[0])
    load.start()
    stacked[...] = jnp.zeros_like(stacked)
    sort_entries(held, number, row, count, order, sems.at[1], keeper, npno * npao // LANES)
    load.wait()
    for o in range(keeper):
        n = count[o]

        def block(b, _):
            ids = [
                order[o * items + jnp.minimum(b * TOGETHER + t, n - 1)] for t in range(TOGETHER)
            ]
            value = lax.dot_general(
                stack(stacked, held, ids, npno),
                blocks[o],
                (((1,), (1,)), ((), ())),
                preferred_element_type=jnp.float32,
            ).astype(out.dtype)
            for t, e in enumerate(ids):
                halves[e, :npno] = value[t * deep : t * deep + npno]
            return 0

        lax.fori_loop(0, (n + TOGETHER - 1) // TOGETHER, block, 0)

    def join(e, _):
        halves[e, npno:] = rest[e]
        return 0

    lax.fori_loop(0, items, join, 0, unroll=8)
    back = pltpu.make_async_copy(halves, out, sems.at[2])
    back.start()
    back.wait()


def far_halves(record, ints, rest, npno):
    keeper, naux, npao = ints.shape
    items, tail, _ = rest.shape
    hbm = pl.BlockSpec(memory_space=pltpu.HBM)
    vmem = pl.BlockSpec(memory_space=pltpu.VMEM)
    return pl.pallas_call(
        functools.partial(far_kernel, npno),
        out_shape=jax.ShapeDtypeStruct((items, npno + tail, naux), jnp.bfloat16),
        in_specs=[vmem, hbm, vmem],
        out_specs=hbm,
        scratch_shapes=[
            pltpu.SMEM(((keeper + 1) * items,), jnp.int32),
            pltpu.SMEM((keeper + 1,), jnp.int32),
            pltpu.VMEM((SPARE, LANES), jnp.int32),
            pltpu.SMEM((SPARE, LANES), jnp.int32),
            pltpu.VMEM((TOGETHER, -(-npno // 16) * 16, npao), jnp.bfloat16),
            pltpu.VMEM(ints.shape, jnp.bfloat16),
            pltpu.VMEM((items, npno + tail, naux), jnp.bfloat16),
            pltpu.SemaphoreType.DMA((3,)),
        ],
        compiler_params=pltpu.CompilerParams(vmem_limit_bytes=48 * 2**20),
        cost_estimate=pl.CostEstimate(
            flops=16 * items * npno * npao * naux,
            bytes_accessed=2 * (keeper * npao * naux + items * npno * (npao + naux)),
            transcendentals=0,
        ),
        name="far",
    )(record, ints, rest)


def hold_kernel(above_in, below_in, above, below):
    pass


def hold(above, below):
    hbm = pl.BlockSpec(memory_space=pltpu.HBM)
    return pl.pallas_call(
        hold_kernel,
        out_shape=[jax.ShapeDtypeStruct(above.shape, above.dtype)] * 2,
        in_specs=[hbm] * 2,
        out_specs=[hbm] * 2,
        input_output_aliases={0: 0, 1: 1},
        compiler_params=pltpu.CompilerParams(vmem_limit_bytes=60 * 2**20),
        cost_estimate=pl.CostEstimate(flops=10**11, bytes_accessed=0, transcendentals=0),
        name="hold",
    )(above, below)


def exchange_kernel(place, first, above, last, below, *refs):
    planes = len(refs) - 4
    outs, (halves, late, product, sems) = refs[:planes], refs[planes:]
    owners, main, _ = first.shape
    npno = halves.shape[1]
    copies = [
        pltpu.make_async_copy(last, late, sems.at[0]),
        pltpu.make_async_copy(
            first, halves.at[pl.ds(0, owners), pl.ds(0, main)], sems.at[1]
        ),
        pltpu.make_async_copy(above, halves.at[pl.ds(owners, owners)], sems.at[2]),
        pltpu.make_async_copy(below, halves.at[pl.ds(3 * owners, owners)], sems.at[3]),
    ]
    for copy in copies:
        copy.start()
    copies[0].wait()

    def join(e, _):
        halves[e, main:] = late[e, npno:]
        halves[2 * owners + e] = late[e, :npno]
        return 0

    lax.fori_loop(0, owners, join, 0, unroll=4)
    for copy in copies[1:]:
        copy.wait()
    each = outs[0].shape[0]

    def some(g, _):
        for k in range(each):
            q = g * each + k
            at = pl.multiple_of(q * npno, 8)
            product[pl.ds(at, npno), :npno] = lax.dot_general(
                halves[place[2 * q]],
                halves[place[2 * q + 1]],
                (((1,), (1,)), ((), ())),
                preferred_element_type=jnp.float32,
            )
        return 0

    lax.fori_loop(0, planes, some, 0)
    for g in range(planes):
        for x in range(npno):
            rows = product[pl.ds(g * each * npno + x, each, stride=npno), :]
            outs[g][:, x * npno : (x + 1) * npno] = rows[:, :npno]


def exchange_of(place, planes, first, above, last, below):
    owners, npno, naux = above.shape
    pairs = place.shape[0] // 2
    hbm = pl.BlockSpec(memory_space=pltpu.HBM)
    vmem = pl.BlockSpec(memory_space=pltpu.VMEM)
    out = jax.ShapeDtypeStruct((pairs // planes, npno * npno), jnp.float32)
    return pl.pallas_call(
        exchange_kernel,
        out_shape=[out] * planes,
        in_specs=[pl.BlockSpec(memory_space=pltpu.SMEM)] + [hbm] * 4,
        out_specs=[vmem] * planes,
        scratch_shapes=[
            pltpu.VMEM((CAP * owners, npno, naux), jnp.bfloat16),
            pltpu.VMEM(last.shape, jnp.bfloat16),
            pltpu.VMEM((pairs * npno, LANES), jnp.float32),
            pltpu.SemaphoreType.DMA((4,)),
        ],
        compiler_params=pltpu.CompilerParams(vmem_limit_bytes=46 * 2**20),
        name="exchange",
    )(place, first, above, last, below)


def body(
    ints_block,
    pair_vectors,
    pair_orbitals,
    orbital_place,
    amplitudes,
    pno_energy,
    occupied_fock_diagonal,
):
    n_orb = lax.axis_size("orb")
    n_rep = lax.axis_size("rep")
    rep = lax.axis_index("rep")
    at = [lax.axis_index(name).reshape(1).astype(jnp.int32) for name in ("rep", "orb")]
    keeper, naux, npao = ints_block.shape
    pair_dev = pair_vectors.shape[0]
    npno = pair_vectors.shape[2]
    vectors = pair_vectors.reshape(2 * pair_dev, npno, npao)

    def shifted(value, by):
        return lax.ppermute(value, "rep", [(i, (i + by) % n_rep) for i in range(n_rep)])

    def there(value):
        return lax.all_to_all(value, "orb", split_axis=0, concat_axis=0, tiled=True)

    sent, slot = route(
        pair_orbitals.T, orbital_place, at, vectors, n_orb, keeper
    )
    own = there(sent)

    above, below = hold(shifted(ints_block, n_rep - 1), shifted(ints_block, 1))
    own, above, below = lax.optimization_barrier((own, above, below))
    opposite = shifted(own, 2)

    near, rest = near_halves(own, ints_block, above, below, npno)
    near = there(near)
    last, near = lax.optimization_barrier((far_halves(opposite, ints_block, rest, npno), near))
    last = there(last)

    main = npno // 16 * 16
    first = near[:, :main]
    above = shifted(near[:, main + npno :], n_rep - 1)
    below = shifted(near[:, main : main + npno], 1)
    place = (slot // n_orb - rep) % n_rep * n_orb + slot % n_orb
    mine = pair_dev // n_rep
    own_orbs = lax.dynamic_slice_in_dim(pair_orbitals, rep * mine, mine, 0)
    first_fock = occupied_fock_diagonal[own_orbs[:, 0]]
    second_fock = occupied_fock_diagonal[own_orbs[:, 1]]
    gap = pno_energy[:, :, None] + pno_energy[:, None, :] - (first_fock + second_fock)[:, None, None]
    local = gap.reshape(mine, npno * npno) * amplitudes.astype(jnp.float32)
    last, local = lax.optimization_barrier((last, local))
    place = jnp.roll(place.reshape(n_rep, 2 * mine), -rep, axis=0).reshape(-1)
    products = exchange_of(place, n_rep, first, above, last, below)
    exchange = products[0]
    for by in (2, 1, n_rep - 1):
        exchange = exchange + shifted(products[by], by)
    return exchange + local


def solution(mesh):
    placed = (
        P("orb", "rep", None),
        P("orb", None, None, None),
        P("orb", None),
        P(),
        P(("orb", "rep"), None),
        P(("orb", "rep"), None),
        P(),
    )
    return jax.shard_map(
        body, mesh=mesh, in_specs=placed, out_specs=P(("orb", "rep"), None), check_vma=False
    )
```

```python
import functools

import jax
import jax.numpy as jnp
from jax import lax
from jax.experimental import pallas as pl
from jax.experimental.pallas import tpu as pltpu
from jax.sharding import PartitionSpec as P

CAP = 4
TOGETHER = 8
SIZES = (8, 12)


LANES = 128
SPARE = 8
PARTS = 4


def pieces(npno, npao):
    whole = npno // 16 * 16
    blocks = npao // LANES
    cuts = []
    for c in range(blocks):
        lanes = slice(c * LANES, (c + 1) * LANES)
        cuts.append((slice(0, whole), lanes, slice(c * whole, (c + 1) * whole)))
        if npno > whole:
            at = blocks * whole + c * (npno - whole)
            cuts.append((slice(whole, npno), lanes, slice(at, at + npno - whole)))
    return cuts


def parted(at, keeper):
    if keeper & (keeper - 1):
        return lax.div(at, keeper), lax.rem(at, keeper)
    return lax.shift_right_logical(at, keeper.bit_length() - 1), lax.bitwise_and(at, keeper - 1)


def route_kernel(
    keeper, orbitals, place, plane, source, vectors, sent, slot, count, row, held, record, sems
):
    owners, npno, npao = held.shape
    pairs = orbitals.shape[1]
    together = 8

    def clear(o, _):
        count[o] = 0
        row[o] = keeper
        return 0

    lax.fori_loop(0, owners, clear, 0, unroll=16)
    mine, turn = plane[0], source[0]

    def fetch(e, owner):
        return pltpu.make_async_copy(vectors.at[e], held.at[owner], sems.at[0])

    def some(g, _):
        for k in range(together):
            q = g * together + k
            for side in range(2):
                owner, of = parted(place[orbitals[side, q]], keeper)
                position = count[owner]
                count[owner] = position + 1
                turned = parted(position + owner + turn, CAP)[1]
                slot[q * 2 + side] = turned * owners + owner

                @pl.when(turned == mine)
                def _():
                    row[owner] = of
                    fetch(q * 2 + side, owner).start()

        return 0

    lax.fori_loop(0, pairs // together, some, 0)

    def arrive(o, _):
        @pl.when(row[o] < keeper)
        def _():
            fetch(0, 0).wait()

        return 0

    lax.fori_loop(0, owners, arrive, 0, unroll=8)

    def lay(o, _):
        for rows, lanes, at in pieces(npno, npao):
            record[o, at, :] = held[o, rows, lanes]
        number = jnp.full((SPARE, LANES), row[o], jnp.int32).astype(jnp.float32)
        record[o, npno * npao // LANES :, :] = number.astype(record.dtype)
        return 0

    outs = []
    for part in range(PARTS):
        own = pl.ds(part * owners // PARTS, owners // PARTS)
        lax.fori_loop(part * owners // PARTS, (part + 1) * owners // PARTS, lay, 0, unroll=2)
        outs.append(pltpu.make_async_copy(record.at[own], sent.at[own], sems.at[1 + part]))
        outs[-1].start()
    for out in outs:
        out.wait()


def route(orbitals, orbital_place, at, vectors, owners, keeper):
    entries, npno, npao = vectors.shape
    depth = npno * npao // LANES + SPARE
    smem = pl.BlockSpec(memory_space=pltpu.SMEM)
    hbm = pl.BlockSpec(memory_space=pltpu.HBM)
    return pl.pallas_call(
        functools.partial(route_kernel, keeper),
        out_shape=(
            jax.ShapeDtypeStruct((owners, depth, LANES), vectors.dtype),
            jax.ShapeDtypeStruct((entries,), jnp.int32),
        ),
        in_specs=[smem] * 4 + [hbm],
        out_specs=(hbm, smem),
        scratch_shapes=[
            pltpu.SMEM((owners,), jnp.int32),
            pltpu.SMEM((owners,), jnp.int32),
            pltpu.VMEM((owners, npno, npao), vectors.dtype),
            pltpu.VMEM((owners, depth, LANES), vectors.dtype),
            pltpu.SemaphoreType.DMA((1 + PARTS,)),
        ],
        compiler_params=pltpu.CompilerParams(vmem_limit_bytes=60 * 2**20),
        name="route",
    )(orbitals, orbital_place, *at, vectors)


def sort_entries(held, number, row, count, order, sem, keeper, at):
    items = held.shape[0]
    tile = held[:, at:, :].astype(jnp.float32)
    own = lax.broadcasted_iota(jnp.int32, tile.shape, 0)
    lane = lax.broadcasted_iota(jnp.int32, tile.shape, 2)
    number[...] = jnp.sum(jnp.where(own == lane, tile, 0.0), axis=0).astype(jnp.int32)
    move = pltpu.make_async_copy(number, row, sem)
    move.start()
    move.wait()
    for o in range(keeper + 1):
        count[o] = 0

    def sort(e, _):
        o = row[0, e]
        n = count[o]
        order[o * items + n] = e
        count[o] = n + 1
        return 0

    lax.fori_loop(0, items, sort, 0, unroll=8)


def stack(stacked, held, ids, npno):
    npao = stacked.shape[2]
    for t, e in enumerate(ids):
        for rows, lanes, at in pieces(npno, npao):
            stacked[t, rows, lanes] = held[e, at, :]
    return stacked[...].reshape(-1, npao)


def near_kernel(
    npno, held, own, above, below, out, rest_out,
    order, count, number, row, stacked, blocks, halves, rest, sems,
):
    keeper, naux, npao = own.shape
    items, tail, _ = rest.shape
    main = npno - tail

    def loads(o):
        return [
            pltpu.make_async_copy(
                share.at[o], blocks.at[o, pl.ds(k * naux, naux)], sems.at[4 + 3 * o + k]
            )
            for k, share in enumerate((own, above, below))
        ]

    for o in range(keeper):
        for load in loads(o):
            load.start()
    sort_entries(held, number, row, count, order, sems.at[1], keeper, npno * npao // LANES)

    def goes(e):
        return pltpu.make_async_copy(halves.at[e], out.at[e], sems.at[2])

    def orbital(o, _):
        for load in loads(o):
            load.wait()
        n = count[o]

        def block(first, size):
            at = [first + t for t in range(size)]
            ids = [order[o * items + jnp.minimum(k, n - 1)] for k in at]
            for t, e in enumerate(ids):
                for rows, lanes, place in pieces(npno, npao):
                    stacked[t * npno + rows.start : t * npno + rows.stop, lanes] = held[e, place, :]
            value = lax.dot_general(
                stacked[: size * npno],
                blocks[o],
                (((1,), (1,)), ((), ())),
                preferred_element_type=jnp.float32,
            )
            for t, e in enumerate(ids):
                rows = value[t * npno : (t + 1) * npno].astype(out.dtype)
                halves[e, :main] = rows[:main, :naux]
                rest[e] = rows[main:, :naux]
                halves[e, main : main + npno] = rows[:, naux : 2 * naux]
                halves[e, main + npno :] = rows[:, 2 * naux :]
            for k, e in zip(at, ids):

                @pl.when(k < n)
                def _():
                    goes(e).start()

        most = SIZES[-1]
        if len(SIZES) == 1:

            def wide(b, _):
                block(b * most, most)
                return 0

            lax.fori_loop(0, (n + most - 1) // most, wide, 0)
        else:
            whole = (n + most - SIZES[0] - 1) // most

            def wide(b, _):
                block(b * most, most)
                return 0

            lax.fori_loop(0, whole, wide, 0)

            @pl.when(n > whole * most)
            def _():
                block(whole * most, SIZES[0])

        return 0

    lax.fori_loop(0, keeper, orbital, 0)

    back = pltpu.make_async_copy(rest, rest_out, sems.at[3])
    back.start()

    def arrive(e, _):
        goes(0).wait()
        return 0

    lax.fori_loop(0, items - count[keeper], arrive, 0)
    back.wait()


def near_halves(record, own, above, below, npno):
    keeper, naux, npao = own.shape
    items = record.shape[0]
    tail = npno % 16
    rows = 3 * npno - tail
    hbm = pl.BlockSpec(memory_space=pltpu.HBM)
    return pl.pallas_call(
        functools.partial(near_kernel, npno),
        out_shape=[
            jax.ShapeDtypeStruct((items, rows, naux), jnp.bfloat16),
            jax.ShapeDtypeStruct((items, tail, naux), jnp.bfloat16),
        ],
        in_specs=[pl.BlockSpec(memory_space=pltpu.VMEM)] + [hbm] * 3,
        out_specs=[hbm] * 2,
        scratch_shapes=[
            pltpu.SMEM(((keeper + 1) * items,), jnp.int32),
            pltpu.SMEM((keeper + 1,), jnp.int32),
            pltpu.VMEM((SPARE, LANES), jnp.int32),
            pltpu.SMEM((SPARE, LANES), jnp.int32),
            pltpu.VMEM((SIZES[-1] * npno, npao), jnp.bfloat16),
            pltpu.VMEM((keeper, 3 * naux, npao), jnp.bfloat16),
            pltpu.VMEM((items, rows, naux), jnp.bfloat16),
            pltpu.VMEM((items, tail, naux), jnp.bfloat16),
            pltpu.SemaphoreType.DMA((4 + 3 * keeper,)),
        ],
        compiler_params=pltpu.CompilerParams(vmem_limit_bytes=48 * 2**20),
        cost_estimate=pl.CostEstimate(
            flops=6 * items * npno * npao * naux,
            bytes_accessed=2 * (3 * keeper * npao * naux + items * npno * (npao + 3 * naux)),
            transcendentals=0,
        ),
        name="near",
    )(record, own, above, below)


def far_kernel(
    npno, held, ints, rest, out, order, count, number, row, stacked, blocks, halves, sems
):
    keeper, naux, npao = ints.shape
    items = held.shape[0]
    deep = stacked.shape[1]
    load = pltpu.make_async_copy(ints, blocks, sems.at[0])
    load.start()
    stacked[...] = jnp.zeros_like(stacked)
    sort_entries(held, number, row, count, order, sems.at[1], keeper, npno * npao // LANES)
    load.wait()
    for o in range(keeper):
        n = count[o]

        def block(b, _):
            ids = [
                order[o * items + jnp.minimum(b * TOGETHER + t, n - 1)] for t in range(TOGETHER)
            ]
            value = lax.dot_general(
                stack(stacked, held, ids, npno),
                blocks[o],
                (((1,), (1,)), ((), ())),
                preferred_element_type=jnp.float32,
            ).astype(out.dtype)
            for t, e in enumerate(ids):
                halves[e, :npno] = value[t * deep : t * deep + npno]
            return 0

        lax.fori_loop(0, (n + TOGETHER - 1) // TOGETHER, block, 0)

    def join(e, _):
        halves[e, npno:] = rest[e]
        return 0

    lax.fori_loop(0, items, join, 0, unroll=8)
    back = pltpu.make_async_copy(halves, out, sems.at[2])
    back.start()
    back.wait()


def far_halves(record, ints, rest, npno):
    keeper, naux, npao = ints.shape
    items, tail, _ = rest.shape
    hbm = pl.BlockSpec(memory_space=pltpu.HBM)
    vmem = pl.BlockSpec(memory_space=pltpu.VMEM)
    return pl.pallas_call(
        functools.partial(far_kernel, npno),
        out_shape=jax.ShapeDtypeStruct((items, npno + tail, naux), jnp.bfloat16),
        in_specs=[vmem, hbm, vmem],
        out_specs=hbm,
        scratch_shapes=[
            pltpu.SMEM(((keeper + 1) * items,), jnp.int32),
            pltpu.SMEM((keeper + 1,), jnp.int32),
            pltpu.VMEM((SPARE, LANES), jnp.int32),
            pltpu.SMEM((SPARE, LANES), jnp.int32),
            pltpu.VMEM((TOGETHER, -(-npno // 16) * 16, npao), jnp.bfloat16),
            pltpu.VMEM(ints.shape, jnp.bfloat16),
            pltpu.VMEM((items, npno + tail, naux), jnp.bfloat16),
            pltpu.SemaphoreType.DMA((3,)),
        ],
        compiler_params=pltpu.CompilerParams(vmem_limit_bytes=48 * 2**20),
        cost_estimate=pl.CostEstimate(
            flops=16 * items * npno * npao * naux,
            bytes_accessed=2 * (keeper * npao * naux + items * npno * (npao + naux)),
            transcendentals=0,
        ),
        name="far",
    )(record, ints, rest)


def hold_kernel(above_in, below_in, above, below):
    pass


def hold(above, below):
    hbm = pl.BlockSpec(memory_space=pltpu.HBM)
    return pl.pallas_call(
        hold_kernel,
        out_shape=[jax.ShapeDtypeStruct(above.shape, above.dtype)] * 2,
        in_specs=[hbm] * 2,
        out_specs=[hbm] * 2,
        input_output_aliases={0: 0, 1: 1},
        compiler_params=pltpu.CompilerParams(vmem_limit_bytes=60 * 2**20),
        cost_estimate=pl.CostEstimate(flops=10**11, bytes_accessed=0, transcendentals=0),
        name="hold",
    )(above, below)


def exchange_kernel(place, near, above, late, below, *refs):
    planes = len(refs) - 3
    outs, (halves, product, sems) = refs[:planes], refs[planes:]
    owners, npno, _ = above.shape
    main = npno // 16 * 16
    copies = [
        pltpu.make_async_copy(above, halves.at[pl.ds(owners, owners)], sems.at[0]),
        pltpu.make_async_copy(below, halves.at[pl.ds(3 * owners, owners)], sems.at[1]),
        pltpu.make_async_copy(
            near.at[:, pl.ds(0, main)], halves.at[pl.ds(0, owners), pl.ds(0, main)], sems.at[2]
        ),
    ]
    for copy in copies:
        copy.start()

    def join(e, _):
        halves[e, main:] = late[e, npno:]
        halves[2 * owners + e] = late[e, :npno]
        return 0

    lax.fori_loop(0, owners, join, 0, unroll=4)
    for copy in copies:
        copy.wait()
    each = outs[0].shape[0]

    def some(g, _):
        for k in range(each):
            q = g * each + k
            at = pl.multiple_of(q * npno, 8)
            product[pl.ds(at, npno), :npno] = lax.dot_general(
                halves[place[2 * q]],
                halves[place[2 * q + 1]],
                (((1,), (1,)), ((), ())),
                preferred_element_type=jnp.float32,
            )
        return 0

    lax.fori_loop(0, planes, some, 0)
    for g in range(planes):
        for x in range(npno):
            rows = product[pl.ds(g * each * npno + x, each, stride=npno), :]
            outs[g][:, x * npno : (x + 1) * npno] = rows[:, :npno]


def exchange_of(place, planes, near, above, last, below):
    owners, npno, naux = above.shape
    pairs = place.shape[0] // 2
    hbm = pl.BlockSpec(memory_space=pltpu.HBM)
    vmem = pl.BlockSpec(memory_space=pltpu.VMEM)
    out = jax.ShapeDtypeStruct((pairs // planes, npno * npno), jnp.float32)
    return pl.pallas_call(
        exchange_kernel,
        out_shape=[out] * planes,
        in_specs=[pl.BlockSpec(memory_space=pltpu.SMEM)] + [hbm, hbm, vmem, hbm],
        out_specs=[vmem] * planes,
        scratch_shapes=[
            pltpu.VMEM((CAP * owners, npno, naux), jnp.bfloat16),
            pltpu.VMEM((pairs * npno, LANES), jnp.float32),
            pltpu.SemaphoreType.DMA((3,)),
        ],
        compiler_params=pltpu.CompilerParams(vmem_limit_bytes=46 * 2**20),
        name="exchange",
    )(place, near, above, last, below)


def body(
    ints_block,
    pair_vectors,
    pair_orbitals,
    orbital_place,
    amplitudes,
    pno_energy,
    occupied_fock_diagonal,
):
    n_orb = lax.axis_size("orb")
    n_rep = lax.axis_size("rep")
    rep = lax.axis_index("rep")
    at = [lax.axis_index(name).reshape(1).astype(jnp.int32) for name in ("rep", "orb")]
    keeper, naux, npao = ints_block.shape
    pair_dev = pair_vectors.shape[0]
    npno = pair_vectors.shape[2]
    vectors = pair_vectors.reshape(2 * pair_dev, npno, npao)

    def shifted(value, by):
        return lax.ppermute(value, "rep", [(i, (i + by) % n_rep) for i in range(n_rep)])

    def there(value):
        return lax.all_to_all(value, "orb", split_axis=0, concat_axis=0, tiled=True)

    sent, slot = route(
        pair_orbitals.T, orbital_place, at, vectors, n_orb, keeper
    )
    own = there(sent)

    above, below = hold(shifted(ints_block, n_rep - 1), shifted(ints_block, 1))
    own, above, below = lax.optimization_barrier((own, above, below))
    opposite = shifted(own, 2)

    near, rest = near_halves(own, ints_block, above, below, npno)
    near = there(near)
    last, near = lax.optimization_barrier((far_halves(opposite, ints_block, rest, npno), near))
    last = there(last)

    main = npno // 16 * 16
    above = shifted(near[:, main + npno :], n_rep - 1)
    below = shifted(near[:, main : main + npno], 1)
    place = (slot // n_orb - rep) % n_rep * n_orb + slot % n_orb
    mine = pair_dev // n_rep
    own_orbs = lax.dynamic_slice_in_dim(pair_orbitals, rep * mine, mine, 0)
    first_fock = occupied_fock_diagonal[own_orbs[:, 0]]
    second_fock = occupied_fock_diagonal[own_orbs[:, 1]]
    gap = pno_energy[:, :, None] + pno_energy[:, None, :] - (first_fock + second_fock)[:, None, None]
    local = gap.reshape(mine, npno * npno) * amplitudes.astype(jnp.float32)
    last, local = lax.optimization_barrier((last, local))
    place = jnp.roll(place.reshape(n_rep, 2 * mine), -rep, axis=0).reshape(-1)
    products = exchange_of(place, n_rep, near, above, last, below)
    exchange = products[0]
    for by in (2, 1, n_rep - 1):
        exchange = exchange + shifted(products[by], by)
    return exchange + local


def solution(mesh):
    placed = (
        P("orb", "rep", None),
        P("orb", None, None, None),
        P("orb", None),
        P(),
        P(("orb", "rep"), None),
        P(("orb", "rep"), None),
        P(),
    )
    return jax.shard_map(
        body, mesh=mesh, in_specs=placed, out_specs=P(("orb", "rep"), None), check_vma=False
    )
```
